128 devices in a mesh: tm: 16 (over y, z_hi, core), space: 8 (over x, z_lo).
Axes of the slice: x: 4, y: 4, z: 4 (z_hi: 2, z_lo: 2; z = z_hi * 2 + z_lo), core: 2. Of those that a mesh axis runs over, the one named last changes fastest.
Arguments:
- guess: float32 [64, 256, 4096], P('tm', 'space'), may hold values from -6 to 6
- forcing: float32 [64, 256, 4096], P('tm', 'space'), may hold values from -4 to 4
- initial: float32 [256, 4096], P('space'), may hold values from -6 to 6
- courant_rows: float32 [256, 4096], P('space'), may hold values from -0.12 to 0.12
- courant_cols: float32 [256, 4096], P('space'), may hold values from -0.12 to 0.12
- diffusion: float32 [256, 4096], P('space'), may hold values from 0.03 to 0.06
Outputs:
- states: float32 [64, 256, 4096], P('tm', 'space')
The draws below stay inside these ranges and needn't reach their ends.
All inputs are finite; a program needn't handle non-finite values.
Results may differ from the reference program's by a relative error of at most 0.00002.
Values sent between devices are 32-bit elements; how exact they have to be, the bound alone decides.
No kernel may reach another device: no remote copies, remote signals or barrier semaphores. Data moves between devices by JAX's collectives and lax.ppermute only.
A program may use at most 64 MiB of HBM per device.

```python
import jax
import jax.numpy as jnp

COLS = 4096
STEPS_DEV = 4
ROWS = 256
NSTEPS = 64


def draw_courant_rows(key, part):
    magnitude = jax.random.uniform(jax.random.fold_in(key, 11), (ROWS, COLS), jnp.float32, 0.06, 0.12)
    return magnitude


def draw_diffusion(key, part):
    exponent = jax.random.uniform(jax.random.fold_in(key, 23), (ROWS, COLS), jnp.float32, jnp.log(0.03), jnp.log(0.06))
    return jnp.clip(jnp.exp(exponent), 0.03, 0.06)


def levels(key, extent, split, least, largest):
    def one(dim, shards_of):
        steps = jax.random.uniform(jax.random.fold_in(jax.random.fold_in(key, 6), dim), (shards_of,), jnp.float32, least / len(split), largest / len(split))
        return jnp.repeat(jnp.exp(steps), extent[dim] // shards_of).reshape((-1,) + (1,) * (len(extent) - dim - 1))

    level = one(*split[0])
    for cut in split[1:]:
        level = level * one(*cut)
    return level


def normal_values(own_key, extent, scale, bound, pieces=(), kind=jnp.bfloat16):
    entries = scale * jax.random.normal(own_key, extent, jnp.float32)
    if pieces:
        entries = entries * levels(own_key, extent, pieces, -0.22, 0.18)
    return jnp.clip(entries, -bound, bound).astype(kind)


def setup_inputs(seed: int = 0) -> dict:
    arg_keys = jax.random.split(jax.random.key(seed), 7)
    guess = normal_values(arg_keys[0], (NSTEPS, ROWS, COLS), 1.0, 6.0, ((0, 16), (1, 8)), jnp.float32)
    forcing = normal_values(arg_keys[1], (NSTEPS, ROWS, COLS), 0.5, 4.0, ((0, 16), (1, 8)), jnp.float32)
    initial = normal_values(arg_keys[2], (ROWS, COLS), 1.0, 6.0, ((0, 8),), jnp.float32)
    courant_rows = draw_courant_rows(jax.random.fold_in(arg_keys[6], 71), 0)
    courant_cols = jnp.clip(jax.random.uniform(arg_keys[4], (ROWS, COLS), jnp.float32, -0.12, 0.12) * levels(arg_keys[4], (ROWS, COLS), ((0, 8),), -0.4, 0.0), -0.12, 0.12)
    diffusion = draw_diffusion(jax.random.fold_in(arg_keys[6], 71), 0)
    return {"guess": guess, "forcing": forcing, "initial": initial, "courant_rows": courant_rows, "courant_cols": courant_cols, "diffusion": diffusion}


def stencil(field, rate_rows, rate_cols, spread):
    padded = jnp.pad(field, ((1, 1), (0, 0)))
    upper = padded[:-2]
    lower = padded[2:]
    left = jnp.roll(field, 1, axis=1)
    right = jnp.roll(field, -1, axis=1)
    advect = jnp.maximum(rate_rows, 0.0) * (field - upper) + jnp.minimum(rate_rows, 0.0) * (lower - field)
    advect = advect + jnp.maximum(rate_cols, 0.0) * (field - left) + jnp.minimum(rate_cols, 0.0) * (right - field)
    laplace = upper + lower + left + right - 4.0 * field
    return field - advect + spread * laplace


def reference(guess, forcing, initial, courant_rows, courant_cols, diffusion):
    steps_dev = STEPS_DEV
    count = guess.shape[0] // steps_dev
    guess_blocks = guess.reshape(count, steps_dev, guess.shape[1], guess.shape[2])
    force_blocks = forcing.reshape(count, steps_dev, guess.shape[1], guess.shape[2])
    residuals = []
    for block in range(count):
        current = initial if block == 0 else guess_blocks[block - 1, steps_dev - 1]
        for inner in range(steps_dev):
            current = stencil(current, courant_rows, courant_cols, diffusion) + force_blocks[block, inner]
        residuals.append(current - guess_blocks[block, steps_dev - 1])
    correction = jnp.zeros_like(initial)
    corrected = []
    for block in range(count):
        for inner in range(steps_dev // 2):
            correction = stencil(correction, 2.0 * courant_rows, 2.0 * courant_cols, 2.0 * diffusion)
        correction = correction + residuals[block]
        corrected.append(guess_blocks[block, steps_dev - 1] + correction)
    outputs = []
    for block in range(count):
        current = initial if block == 0 else corrected[block - 1]
        for inner in range(steps_dev - 1):
            current = stencil(current, courant_rows, courant_cols, diffusion) + force_blocks[block, inner]
            outputs.append(current)
        outputs.append(corrected[block])
    return jnp.stack(outputs)
```

```python
import jax
import jax.numpy as jnp
from jax import lax
from jax.experimental import pallas as pl
from jax.experimental.pallas import tpu as pltpu
from jax.sharding import Mesh, PartitionSpec as P

ROWS = 32
LANES = 128
HALO = 32
VMEM = pl.BlockSpec(memory_space=pltpu.VMEM)
SMEM = pl.BlockSpec(memory_space=pltpu.SMEM)
F32 = jnp.float32
RIM = ((0, 3), (3, 3), (6, 3), (9, 3), (12, 2), (14, 1))


def params(mib):
    return pltpu.CompilerParams(vmem_limit_bytes=mib * 1024 * 1024)


def iota(dim):
    return lax.broadcasted_iota(jnp.int32, (8, LANES), dim)


def cols(j):
    return slice(LANES * j, LANES * (j + 1))


def tile(r, first=0):
    return slice(first + 8 * r, first + 8 * r + 8)


def rates(a, b, d):
    a_pos, a_neg = jnp.maximum(a, 0.0), jnp.minimum(a, 0.0)
    b_pos, b_neg = jnp.maximum(b, 0.0), jnp.minimum(b, 0.0)
    own = 1.0 - (a_pos - a_neg) - (b_pos - b_neg) - 4.0 * d
    return own, d + a_pos, d - a_neg, d + b_pos, d - b_neg


def put(ref, j, r, value):
    ref[j, tile(r, 8), :] = value
    if r == 4:
        ref[j, 0:8, :] = value


def sweep(ref, coef, rows, use):
    tiles = ref.shape[0]
    lane = iota(1)
    for r in rows:
        at = 8 + 8 * r
        mids, rights, lefts = {}, {}, {}

        def load(j):
            j %= tiles
            if j not in mids:
                mids[j] = ref[j, at : at + 8, :]
                rights[j] = pltpu.roll(mids[j], 1, 1)
                lefts[j] = pltpu.roll(mids[j], LANES - 1, 1)

        for j in range(tiles):
            for i in (j - 1, j, j + 1):
                load(i)
            mid = mids[j]
            up = ref[j, at - 1 : at + 7, :]
            low = ref[j, at + 1 : at + 9, :] if r < 4 else ref[j, 1:9, :]
            left = jnp.where(lane == 0, rights[(j - 1) % tiles], rights[j])
            right = jnp.where(lane == LANES - 1, lefts[(j + 1) % tiles], lefts[j])
            total = coef[0, j, tile(r), :] * mid + coef[1, j, tile(r), :] * up
            total += coef[2, j, tile(r), :] * low + coef[3, j, tile(r), :] * left
            use(j, r, total + coef[4, j, tile(r), :] * right, mid)


def rim_kernel(flag, guess, initial, a, b, d, forcing, last, start_low, start_up, low, up):
    tiles = a.shape[1] // LANES
    at_end = flag[2] == 1
    last[...] = guess[0]
    rows = last.shape[0]
    start_low[...] = jnp.where(at_end, initial[0:4, :], guess[0, 0:4, :])
    start_up[...] = jnp.where(at_end, initial[rows - 4 : rows, :], guess[0, rows - 4 : rows, :])
    sources = [lambda at, j, x=x: x[at, cols(j)] for x in (a, b, d)]
    sources += [lambda at, j, i=i: forcing[i, at, cols(j)] for i in range(3)]
    for j in range(tiles):
        for source, (to, count) in zip(sources, RIM, strict=True):
            low[j, to : to + count, :] = source(slice(0, count), j)
            up[j, to : to + count, :] = source(slice(rows - count, rows), j)
        low[j, 15:16, :] = jnp.zeros((1, LANES), F32)
        up[j, 15:16, :] = jnp.zeros((1, LANES), F32)


def rim_tile(low, up, j, item, sub):
    at, count = RIM[item]
    under = low[j, at : at + 8, :] if at <= 8 else pltpu.roll(low[j, 8:16, :], 16 - at, 0)
    begin = at + count - 8
    over = up[j, begin : begin + 8, :] if begin >= 0 else pltpu.roll(up[j, 0:8, :], -begin, 0)
    return jnp.where(sub < 4, under, over)


def residual_kernel(flag, before, initial, start_low, start_up, low, up, guess, forcing, a, b, d,
                    messages, ends, coef, rims, one, two, three, res):
    tiles = a.shape[1] // LANES
    lane, sub = iota(1), iota(0)
    first = flag[0] == 1
    turn = flag[3]
    for j in range(tiles):
        for r in range(5):
            if r < 4:
                values = a[tile(r), cols(j)], b[tile(r), cols(j)], d[tile(r), cols(j)]
                put(one, j, r, jnp.where(first, initial[tile(r), cols(j)], before[tile(r), cols(j)]))
            else:
                values = [rim_tile(low, up, j, item, sub) for item in range(3)]
                for at in (0, 40):
                    one[j, at : at + 4, :] = start_low[:, cols(j)]
                    one[j, at + 4 : at + 8, :] = start_up[:, cols(j)]
            for i, value in enumerate(rates(*values)):
                coef[i, j, tile(r), :] = value
        for inner in range(3):
            rims[inner, j, :, :] = rim_tile(low, up, j, 3 + inner, sub)

    for inner, (source, target) in enumerate([(one, two), (two, three), (three, two)]):

        def fine(j, r, value, _, inner=inner, target=target):
            put(target, j, r, value + (forcing[inner, tile(r), cols(j)] if r < 4 else rims[inner, j, :, :]))

        sweep(source, coef, range(5), fine)

    def last(j, r, value, _):
        value = value + forcing[3, tile(r), cols(j)]
        ends[j, tile(r), :] = value
        res[j, tile(r), :] = value - guess[tile(r), cols(j)]

    sweep(two, coef, range(4), last)

    for r in range(4):
        for j in range(tiles):
            x, y, z = (res[i % tiles, tile(r), :] for i in (j - 1, j, j + 1))
            messages[2 * j, tile(r), :] = pltpu.roll(jnp.where(lane >= LANES - HALO, x, y), HALO, 1)
            messages[2 * j + 1, tile(r), :] = pltpu.roll(jnp.where(lane < HALO, z, y), LANES - HALO, 1)

    which, row = lax.div(turn, 4), pl.ds(pl.multiple_of(8 * lax.rem(turn, 4), 8), 8)
    for j in range(tiles):
        x, y, z = (
            jnp.where(which == 0, a[row, cols(i % tiles)], jnp.where(which == 1, b[row, cols(i % tiles)], d[row, cols(i % tiles)]))
            for i in (j - 1, j, j + 1)
        )
        messages[2 * j, tile(4), :] = pltpu.roll(jnp.where(lane >= LANES - HALO, x, y), HALO, 1)
        messages[2 * j + 1, tile(4), :] = pltpu.roll(jnp.where(lane < HALO, z, y), LANES - HALO, 1)


def chain_kernel(flag, mine, other, messages, coef, one, two):
    pairs = spaces = 8
    rows = spaces * ROWS
    blocks = rows // 8
    lane, sub = iota(1), iota(0)
    even = flag[1] == 0
    zero = jnp.zeros((8, LANES), F32)

    def arrived(pair, odd, s, r):
        same, across = mine[pair * spaces + s, tile(r), :], other[pair * spaces + s, tile(r), :]
        return jnp.where(even, across, same) if odd else jnp.where(even, same, across)

    for s in range(spaces):
        for r in range(4):
            a, b, d = (arrived((4 * i + r) // 2, r % 2 == 1, s, 4) for i in range(3))
            own, up, low, left, right = rates(a, b, d)
            at = tile(r, s * ROWS)
            coef[0, at, :] = 2.0 * own - 1.0
            for i, value in enumerate((up, low, left, right)):
                coef[i + 1, at, :] = 2.0 * value
    for ref in (one, two):
        ref[0:8, :] = zero
        ref[rows + 8 : rows + 16, :] = zero
    for t in range(blocks):
        one[tile(t, 8), :] = zero

    def step(source, t):
        at = 8 * t + 8
        mid = source[at : at + 8, :]
        total = coef[0, tile(t), :] * mid + coef[1, tile(t), :] * source[at - 1 : at + 7, :]
        total += coef[2, tile(t), :] * source[at + 1 : at + 9, :]
        total += coef[3, tile(t), :] * pltpu.roll(mid, 1, 1)
        return total + coef[4, tile(t), :] * pltpu.roll(mid, LANES - 1, 1)

    def emit(pair):
        for s in range(spaces):
            at = 8 + ROWS * s
            tiles = [one[tile(r, at), :] for r in range(4)]
            rim = jnp.where(sub < 4, one[at + ROWS : at + ROWS + 8, :], one[at - 8 : at, :])
            low = [pltpu.roll(x, LANES - HALO, 1) for x in tiles[:3]]
            high = [pltpu.roll(x, HALO, 1) for x in (tiles[3], rim)]
            where = pair * spaces + s
            messages[where, 0:8, :] = jnp.where(lane < 64, low[0], high[0])
            messages[where, 8:16, :] = jnp.where(lane < 64, low[1], high[1])
            messages[where, 16:24, :] = low[2]

    def advance(pair, odd):
        for t in range(blocks):
            two[tile(t, 8), :] = step(one, t)
        for t in range(blocks):
            one[tile(t, 8), :] = step(two, t) + arrived(pair, odd, t // 4, t % 4)

    def turn(pair, _):
        pl.when(even)(lambda: emit(pair))
        advance(pair, False)
        pl.when(jnp.logical_not(even))(lambda: emit(pair))
        pl.when(pair < pairs - 1)(lambda: advance(pair, True))
        return 0

    lax.fori_loop(0, pairs, turn, 0)


def final_kernel(start, coef, rims, forcing, ends, returned, states, one, two, err, half):
    tiles = start.shape[0]
    lane = iota(1)
    for j in range(tiles):
        for r in range(5):
            x, y = returned[2 * j, tile(r % 3), :], returned[2 * j + 1, tile(r % 3), :]
            if r < 3:
                error = jnp.where(lane < 64, x, pltpu.roll(y, 64, 1))
            else:
                error = jnp.where(lane < 64, pltpu.roll(x, 64, 1), y)
            put(err, j, r, error)
            put(one, j, r, start[j, tile(r, 8), :] + error)

    def coarse(j, r, value, own):
        put(half, j, r, 2.0 * value - own)

    def corrected(j, r, value, own):
        states[3, tile(r), cols(j)] = ends[j, tile(r), :] + (2.0 * value - own)

    def fine(inner, target):
        def use(j, r, value, _):
            value = value + (forcing[inner, tile(r), cols(j)] if r < 4 else rims[inner, j, :, :])
            if r < 4:
                states[inner, tile(r), cols(j)] = value
            if target is not None:
                put(target, j, r, value)

        return use

    sweep(one, coef, range(5), fine(0, two))
    sweep(err, coef, range(5), coarse)
    sweep(two, coef, range(5), fine(1, one))
    sweep(half, coef, range(4), corrected)
    sweep(one, coef, range(4), fine(2, None))


def on_device(guess, forcing, initial, courant_rows, courant_cols, diffusion):
    chips, cores, spaces = (lax.axis_size(n) for n in ("chip", "core", "space"))
    owners = chips * cores
    columns = initial.shape[1]
    tiles = columns // LANES
    everything = ("chip", "core", "space")
    chip, core = lax.axis_index("chip"), lax.axis_index("core")
    turn = chip * cores + core
    flag = jnp.stack([turn == 0, core, turn == owners - 1, turn]).astype(jnp.int32)

    def shaped(*shape):
        return jax.ShapeDtypeStruct(shape, F32)

    def whole(*shape):
        return pl.BlockSpec(shape, lambda i: (0,) * len(shape))

    block = whole(ROWS, columns)
    last, start_low, start_up, low, up = pl.pallas_call(
        rim_kernel,
        grid=(1,),
        in_specs=[SMEM, pl.BlockSpec((1, ROWS, columns), lambda i: (3, 0, 0)), block, block, block, block,
                  whole(3, ROWS, columns)],
        out_specs=[block, whole(4, columns), whole(4, columns), whole(tiles, 16, LANES), whole(tiles, 16, LANES)],
        out_shape=[shaped(ROWS, columns), shaped(4, columns), shaped(4, columns), shaped(tiles, 16, LANES),
                   shaped(tiles, 16, LANES)],
        compiler_params=params(20),
        name="rim",
    )(flag, guess, initial, courant_rows, courant_cols, diffusion, forcing)

    before = lax.ppermute(last, ("chip", "core"), [(i, i + 1) for i in range(owners - 1)])

    def shifted(value, by_turn, by_space):
        pairs = []
        for k in range(owners):
            for s in range(spaces):
                if 0 <= s + by_space < spaces:
                    pairs.append((k * spaces + s, (k + by_turn) % owners * spaces + s + by_space))
        return lax.ppermute(value, everything, pairs)

    start_up, start_low = shifted(start_up, 1, 1), shifted(start_low, 1, -1)
    up, low = shifted(up, 0, 1), shifted(low, 0, -1)

    field = pltpu.VMEM((tiles, 48, LANES), F32)
    messages, ends, coef, rims, start = pl.pallas_call(
        residual_kernel,
        in_specs=[SMEM] + [VMEM] * 11,
        out_specs=[VMEM] * 5,
        out_shape=[shaped(2 * tiles, 40, LANES), shaped(tiles, ROWS, LANES), shaped(5, tiles, 40, LANES),
                   shaped(3, tiles, 8, LANES), shaped(tiles, 48, LANES)],
        scratch_shapes=[field, field, pltpu.VMEM((tiles, ROWS, LANES), F32)],
        compiler_params=params(20),
        name="residual",
    )(flag, before, initial, start_low, start_up, low, up, last, forcing, courant_rows, courant_cols, diffusion)

    mine = lax.all_to_all(messages, ("chip", "space"), 0, 0, tiled=True)
    other = lax.ppermute(mine, "core", [(0, 1), (1, 0)])
    rows = spaces * ROWS
    answer = pl.pallas_call(
        chain_kernel,
        in_specs=[SMEM, VMEM, VMEM],
        out_specs=VMEM,
        out_shape=shaped(chips * spaces, 24, LANES),
        scratch_shapes=[
            pltpu.VMEM((5, rows, LANES), F32),
            pltpu.VMEM((rows + 16, LANES), F32),
            pltpu.VMEM((rows + 16, LANES), F32),
        ],
        compiler_params=params(20),
        name="chain",
    )(flag, mine, other)
    returned = lax.all_to_all(answer, ("chip", "space"), 0, 0, tiled=True)
    return pl.pallas_call(
        final_kernel,
        in_specs=[VMEM] * 6,
        out_specs=VMEM,
        out_shape=shaped(4, ROWS, columns),
        scratch_shapes=[field, field, field, field],
        compiler_params=params(20),
        name="final",
    )(start, coef, rims, forcing, ends, returned)


def solution(mesh):
    cores = 2
    devices = mesh.devices
    grid = Mesh(
        devices.reshape(devices.shape[0] // cores, cores, devices.shape[1]), ("chip", "core", "space")
    )
    time_rows = P(("chip", "core"), "space", None)
    rows = P("space", None)
    return jax.shard_map(
        on_device,
        mesh=grid,
        in_specs=(time_rows, time_rows, rows, rows, rows, rows),
        out_specs=time_rows,
        check_vma=False,
    )
```

```python
import jax
import jax.numpy as jnp
from jax import lax
from jax.experimental import pallas as pl
from jax.experimental.pallas import tpu as pltpu
from jax.sharding import Mesh, PartitionSpec as P

ROWS = 32
LANES = 128
HALO = 32
VMEM = pl.BlockSpec(memory_space=pltpu.VMEM)
SMEM = pl.BlockSpec(memory_space=pltpu.SMEM)
F32 = jnp.float32
ANY = pl.BlockSpec(memory_space=pl.ANY)
G1, G2, G3, PART, A1, B1, D1, INWARD = range(8)
START1, START2, STEP1, STEP2 = range(4)


def params(mib):
    return pltpu.CompilerParams(vmem_limit_bytes=mib * 1024 * 1024)


def iota(dim):
    return lax.broadcasted_iota(jnp.int32, (8, LANES), dim)


def cols(j):
    return slice(LANES * j, LANES * (j + 1))


def tile(r, first=0):
    return slice(first + 8 * r, first + 8 * r + 8)


def rates(a, b, d):
    a_pos, a_neg = jnp.maximum(a, 0.0), jnp.minimum(a, 0.0)
    b_pos, b_neg = jnp.maximum(b, 0.0), jnp.minimum(b, 0.0)
    own = 1.0 - (a_pos - a_neg) - (b_pos - b_neg) - 4.0 * d
    return own, d + a_pos, d - a_neg, d + b_pos, d - b_neg


def put(ref, j, r, value):
    ref[j, tile(r, 8), :] = value
    if r == 4:
        ref[j, 0:8, :] = value


def sweep(ref, coef, rows, use):
    tiles = ref.shape[0]
    lane = iota(1)
    for r in rows:
        at = 8 + 8 * r
        mids, rights, lefts = {}, {}, {}

        def load(j):
            j %= tiles
            if j not in mids:
                mids[j] = ref[j, at : at + 8, :]
                rights[j] = pltpu.roll(mids[j], 1, 1)
                lefts[j] = pltpu.roll(mids[j], LANES - 1, 1)

        for j in range(tiles):
            for i in (j - 1, j, j + 1):
                load(i)
            mid = mids[j]
            up = ref[j, at - 1 : at + 7, :]
            low = ref[j, at + 1 : at + 9, :] if r < 4 else ref[j, 1:9, :]
            left = jnp.where(lane == 0, rights[(j - 1) % tiles], rights[j])
            right = jnp.where(lane == LANES - 1, lefts[(j + 1) % tiles], lefts[j])
            total = coef[0, j, tile(r), :] * mid + coef[1, j, tile(r), :] * up
            total += coef[2, j, tile(r), :] * low + coef[3, j, tile(r), :] * left
            use(j, r, total + coef[4, j, tile(r), :] * right, mid)


def last_kernel(guess, last, sem):
    copy = pltpu.make_async_copy(guess.at[3], last, sem)
    copy.start()
    copy.wait()


def rim_kernel(flag, guess, initial, a, b, d, forcing, rim_one, rim_two, start_one, start_two,
               va, vi, vg, vc, coef, field, after, sems):
    rows, columns = a.shape
    tiles = columns // LANES
    sub, lane = iota(0), iota(1)
    copies = []
    for side in range(2):
        at = pl.ds(0 if side == 0 else rows - 8, 8)
        moves = [(x.at[at, :], vc.at[i, side]) for i, x in enumerate((a, b, d))]
        moves += [(forcing.at[i, at, :], vg.at[i, side]) for i in range(3)]
        moves += [(guess.at[3, at, :], va.at[side]), (initial.at[at, :], vi.at[side])]
        for source, target in moves:
            copies.append(pltpu.make_async_copy(source, target, sems.at[len(copies)]))
    for copy in copies:
        copy.start()
    for copy in copies:
        copy.wait()
    at_end, even = flag[2] == 1, flag[4] == 0

    def outward(x, side):
        return pltpu.roll(x, 7 if side == 0 else 1, 0)

    def inward(x, side):
        return pltpu.roll(x, 1 if side == 0 else 7, 0)

    def row(x, side, place, to):
        at = place - 1 if side == 0 else 8 - place
        return pltpu.roll(x, (to - at) % 8, 0)

    def open_step(values, j, side):
        x, y, z = (values[i % tiles] for i in (j - 1, j, j + 1))
        left = pltpu.roll(jnp.where(lane == LANES - 1, x, y), 1, 1)
        right = pltpu.roll(jnp.where(lane == 0, z, y), LANES - 1, 1)
        out = coef[side, 2 - side, j]
        return coef[side, 0, j] * y + out * outward(y, side) + coef[side, 3, j] * left + coef[side, 4, j] * right

    class Tiles:
        def __init__(self, get):
            self.get, self.seen = get, {}

        def __getitem__(self, j):
            if j not in self.seen:
                self.seen[j] = self.get(j)
            return self.seen[j]

    for side in range(2):
        for j in range(tiles):
            for i, value in enumerate(rates(*(vc[n, side, :, cols(j)] for n in range(3)))):
                coef[side, i, j] = value
            field[side, j] = jnp.where(at_end, vi[side, :, cols(j)], va[side, :, cols(j)])
    for side in range(2):
        values = Tiles(lambda j, side=side: field[side, j])
        for j in range(tiles):
            part = open_step(values, j, side)
            after[side, 0, j] = part
            after[side, 1, j] = part + coef[side, 1 + side, j] * inward(values[j], side)
    for j in range(tiles):
        rims, starts = [], []
        for side in range(2):
            forced = Tiles(lambda j, side=side: vg[0, side, :, cols(j)])
            stepped = Tiles(lambda j, side=side: after[side, 1, j])
            g1, g2, g3 = (vg[i, side, :, cols(j)] for i in range(3))
            second = g2 + coef[side, 2 - side, j] * outward(g1, side)
            part = open_step(forced, j, side) + g2
            items = [(G1, g1, 1), (G2, second, 1), (G3, g3, 1), (PART, part, 2)]
            items += [(A1 + i, vc[i, side, :, cols(j)], 1) for i in range(3)]
            items += [(INWARD, coef[side, 1 + side, j], 2)]
            total = row(g1, side, 1, 0)
            for to, value, place in items[1:]:
                total = jnp.where(sub == to, row(value, side, place, to), total)
            rims.append(total)
            values = field[side, j]
            total = row(values, side, 1, START1)
            for to, value in ((START2, values), (STEP1, after[side, 0, j]), (STEP2, open_step(stepped, j, side))):
                total = jnp.where(sub == to, row(value, side, 2, to), total)
            starts.append(total[0:4])
        rim_one[j] = jnp.where(even, rims[1], rims[0])
        rim_two[j] = jnp.where(even, rims[0], rims[1])
        start_one[j] = jnp.where(even, starts[1], starts[0])
        start_two[j] = jnp.where(even, starts[0], starts[1])


def residual_kernel(flag, before, initial, start_one, start_two, rim_one, rim_two, guess, forcing, a, b, d,
                    messages, ends, coef, rims, one, two, three, res, edge):
    tiles = a.shape[1] // LANES
    lane, sub = iota(1), iota(0)
    first, even = flag[0] == 1, flag[4] == 0
    turn = flag[3]
    zero = jnp.zeros((8, LANES), F32)
    for j in range(tiles):
        edge[0, j, 0:4, :] = jnp.where(even, start_one[j], start_two[j])
        edge[1, j, 0:4, :] = jnp.where(even, start_two[j], start_one[j])
    for j in range(tiles):
        low, up = jnp.where(even, rim_one[j], rim_two[j]), jnp.where(even, rim_two[j], rim_one[j])
        start_low, start_up = edge[0, j], edge[1, j]

        def border(under, over, item, place=1, rest=zero):
            under = pltpu.roll(under, (place - 1 - item) % 8, 0)
            over = pltpu.roll(over, (8 - place - item) % 8, 0)
            return jnp.where(sub == place - 1, under, jnp.where(sub == 8 - place, over, rest))

        for r in range(4):
            values = a[tile(r), cols(j)], b[tile(r), cols(j)], d[tile(r), cols(j)]
            put(one, j, r, jnp.where(first, initial[tile(r), cols(j)], before[tile(r), cols(j)]))
            for i, value in enumerate(rates(*values)):
                coef[i, j, tile(r), :] = value
        start = border(start_low, start_up, START1)
        put(one, j, 4, border(start_low, start_up, START2, 2, start))
        own, upper, lower, left, right = rates(*(border(low, up, item) for item in (A1, B1, D1)))
        own = jnp.where((sub == 0) | (sub == 7), own, 0.0)
        upper = jnp.where(sub == 1, pltpu.roll(low, (1 - INWARD) % 8, 0), upper)
        lower = jnp.where(sub == 6, pltpu.roll(up, (6 - INWARD) % 8, 0), lower)
        for i, value in enumerate((own, upper, lower, left, right)):
            coef[i, j, tile(4), :] = value
        rims[0, j] = border(start_low, start_up, STEP1, 2, border(low, up, G1))
        rims[1, j] = border(low, up, G2) + border(start_low, start_up, STEP2, 2) + border(low, up, PART, 2)
        rims[2, j] = border(low, up, G3)

    for inner, (source, target) in enumerate([(one, two), (two, three), (three, two)]):

        def fine(j, r, value, _, inner=inner, target=target):
            put(target, j, r, value + (forcing[inner, tile(r), cols(j)] if r < 4 else rims[inner, j]))

        sweep(source, coef, range(5), fine)

    def last(j, r, value, _):
        value = value + forcing[3, tile(r), cols(j)]
        ends[j, tile(r), :] = value
        res[j, tile(r), :] = value - guess[tile(r), cols(j)]

    sweep(two, coef, range(4), last)

    for r in range(4):
        for j in range(tiles):
            x, y, z = (res[i % tiles, tile(r), :] for i in (j - 1, j, j + 1))
            messages[2 * j, tile(r), :] = pltpu.roll(jnp.where(lane >= LANES - HALO, x, y), HALO, 1)
            messages[2 * j + 1, tile(r), :] = pltpu.roll(jnp.where(lane < HALO, z, y), LANES - HALO, 1)

    which, at = lax.div(turn, 4), pl.ds(pl.multiple_of(8 * lax.rem(turn, 4), 8), 8)
    for j in range(tiles):
        x, y, z = (
            jnp.where(which == 0, a[at, cols(i % tiles)], jnp.where(which == 1, b[at, cols(i % tiles)], d[at, cols(i % tiles)]))
            for i in (j - 1, j, j + 1)
        )
        messages[2 * j, tile(4), :] = pltpu.roll(jnp.where(lane >= LANES - HALO, x, y), HALO, 1)
        messages[2 * j + 1, tile(4), :] = pltpu.roll(jnp.where(lane < HALO, z, y), LANES - HALO, 1)


def chain_kernel(flag, mine, other, messages, coef, one, two):
    pairs = spaces = 8
    rows = spaces * ROWS
    blocks = rows // 8
    lane, sub = iota(1), iota(0)
    even = flag[1] == 0
    zero = jnp.zeros((8, LANES), F32)

    def arrived(pair, odd, s, r):
        same, across = mine[pair * spaces + s, tile(r), :], other[pair * spaces + s, tile(r), :]
        return jnp.where(even, across, same) if odd else jnp.where(even, same, across)

    for s in range(spaces):
        for r in range(4):
            a, b, d = (arrived((4 * i + r) // 2, r % 2 == 1, s, 4) for i in range(3))
            own, up, low, left, right = rates(a, b, d)
            at = tile(r, s * ROWS)
            coef[0, at, :] = 2.0 * own - 1.0
            for i, value in enumerate((up, low, left, right)):
                coef[i + 1, at, :] = 2.0 * value
    for ref in (one, two):
        ref[0:8, :] = zero
        ref[rows + 8 : rows + 16, :] = zero
    for t in range(blocks):
        one[tile(t, 8), :] = zero

    def step(source, t):
        at = 8 * t + 8
        mid = source[at : at + 8, :]
        total = coef[0, tile(t), :] * mid + coef[1, tile(t), :] * source[at - 1 : at + 7, :]
        total += coef[2, tile(t), :] * source[at + 1 : at + 9, :]
        total += coef[3, tile(t), :] * pltpu.roll(mid, 1, 1)
        return total + coef[4, tile(t), :] * pltpu.roll(mid, LANES - 1, 1)

    def emit(pair):
        for s in range(spaces):
            at = 8 + ROWS * s
            tiles = [one[tile(r, at), :] for r in range(4)]
            under, over = slice(at + ROWS, at + ROWS + 8), slice(at - 8, at)
            low_step = pltpu.roll(0.5 * (two[under, :] + one[under, :]), 1, 0)
            up_step = pltpu.roll(0.5 * (two[over, :] + one[over, :]), 7, 0)
            rim = jnp.where(sub < 2, one[under, :], one[over, :])
            rim = jnp.where(sub == 2, low_step, jnp.where(sub == 5, up_step, rim))
            low = [pltpu.roll(x, LANES - HALO, 1) for x in tiles[:3]]
            high = [pltpu.roll(x, HALO, 1) for x in (tiles[3], rim)]
            where = pair * spaces + s
            messages[where, 0:8, :] = jnp.where(lane < 64, low[0], high[0])
            messages[where, 8:16, :] = jnp.where(lane < 64, low[1], high[1])
            messages[where, 16:24, :] = low[2]

    def half():
        for t in range(blocks):
            two[tile(t, 8), :] = step(one, t)

    def rest(pair, odd):
        for t in range(blocks):
            one[tile(t, 8), :] = step(two, t) + arrived(pair, odd, t // 4, t % 4)

    def turn(pair, _):
        half()
        pl.when(even)(lambda: emit(pair))
        rest(pair, False)
        half()
        pl.when(jnp.logical_not(even))(lambda: emit(pair))
        pl.when(pair < pairs - 1)(lambda: rest(pair, True))
        return 0

    lax.fori_loop(0, pairs, turn, 0)


def final_kernel(start, coef, rims, forcing, ends, returned, states, one, two, err, half, extra):
    tiles = start.shape[0]
    lane, sub = iota(1), iota(0)
    for j in range(tiles):
        for r in range(5):
            x, y = returned[2 * j, tile(r % 3), :], returned[2 * j + 1, tile(r % 3), :]
            if r < 3:
                error = jnp.where(lane < 64, x, pltpu.roll(y, 64, 1))
            else:
                error = jnp.where(lane < 64, pltpu.roll(x, 64, 1), y)
            put(err, j, r, error)
            put(one, j, r, start[j, tile(r, 8), :] + error)
        after, behind = pltpu.roll(error, 7, 0), pltpu.roll(error, 1, 0)
        under = after - coef[1, j, tile(4), :] * behind
        over = behind - coef[2, j, tile(4), :] * after
        extra[j] = rims[0, j] + jnp.where(sub == 1, under, jnp.where(sub == 6, over, 0.0))

    def coarse(j, r, value, own):
        put(half, j, r, 2.0 * value - own)

    def corrected(j, r, value, own):
        states[3, tile(r), cols(j)] = ends[j, tile(r), :] + (2.0 * value - own)

    def fine(inner, target):
        def use(j, r, value, _):
            beyond = extra if inner == 0 else rims.at[1]
            value = value + (forcing[inner, tile(r), cols(j)] if r < 4 else beyond[j])
            if r < 4:
                states[inner, tile(r), cols(j)] = value
            if target is not None:
                put(target, j, r, value)

        return use

    sweep(one, coef, range(5), fine(0, two))
    sweep(err, coef, range(5), coarse)
    sweep(two, coef, range(5), fine(1, one))
    sweep(half, coef, range(4), corrected)
    sweep(one, coef, range(4), fine(2, None))


def on_device(guess, forcing, initial, courant_rows, courant_cols, diffusion):
    chips, cores, spaces = (lax.axis_size(n) for n in ("chip", "core", "space"))
    owners = chips * cores
    columns = initial.shape[1]
    tiles = columns // LANES
    everything = ("chip", "core", "space")
    chip, core = lax.axis_index("chip"), lax.axis_index("core")
    turn = chip * cores + core
    flag = jnp.stack([turn == 0, core, turn == owners - 1, turn, lax.axis_index("space") % 2]).astype(jnp.int32)

    def shaped(*shape):
        return jax.ShapeDtypeStruct(shape, F32)

    last = pl.pallas_call(
        last_kernel,
        in_specs=[ANY],
        out_specs=VMEM,
        out_shape=shaped(ROWS, columns),
        scratch_shapes=[pltpu.SemaphoreType.DMA],
        compiler_params=params(52),
        name="last",
    )(guess)
    before = lax.ppermute(last, ("chip", "core"), [(i, i + 1) for i in range(owners - 1)])
    small = pltpu.VMEM((2, tiles, 8, LANES), F32)
    edge_rows = pltpu.VMEM((2, 8, columns), F32)
    rim_one, rim_two, start_one, start_two = pl.pallas_call(
        rim_kernel,
        in_specs=[SMEM] + [ANY] * 6,
        out_specs=[VMEM] * 4,
        out_shape=[shaped(tiles, 8, LANES), shaped(tiles, 8, LANES), shaped(tiles, 4, LANES), shaped(tiles, 4, LANES)],
        scratch_shapes=[
            edge_rows,
            edge_rows,
            pltpu.VMEM((3, 2, 8, columns), F32),
            pltpu.VMEM((3, 2, 8, columns), F32),
            pltpu.VMEM((2, 5, tiles, 8, LANES), F32),
            small,
            pltpu.VMEM((2, 2, tiles, 8, LANES), F32),
            pltpu.SemaphoreType.DMA((16,)),
        ],
        compiler_params=params(52),
        name="rim",
    )(flag, guess, initial, courant_rows, courant_cols, diffusion, forcing)

    def exchanged(value, by_turn, first):
        pairs = []
        for k in range(owners):
            for s in range(spaces):
                partner = s + 1 if (s % 2 == 0) == first else s - 1
                if 0 <= partner < spaces:
                    pairs.append((k * spaces + s, (k + by_turn) % owners * spaces + partner))
        return lax.ppermute(value, everything, pairs)

    rim_one, rim_two = exchanged(rim_one, 0, True), exchanged(rim_two, 0, False)
    start_one, start_two = exchanged(start_one, 1, True), exchanged(start_two, 1, False)

    field = pltpu.VMEM((tiles, 48, LANES), F32)
    messages, ends, coef, rims, start = pl.pallas_call(
        residual_kernel,
        in_specs=[SMEM] + [VMEM] * 11,
        out_specs=[VMEM] * 5,
        out_shape=[shaped(2 * tiles, 40, LANES), shaped(tiles, ROWS, LANES), shaped(5, tiles, 40, LANES),
                   shaped(3, tiles, 8, LANES), shaped(tiles, 48, LANES)],
        scratch_shapes=[field, field, pltpu.VMEM((tiles, ROWS, LANES), F32), small],
        compiler_params=params(20),
        name="residual",
    )(flag, before, initial, start_one, start_two, rim_one, rim_two, last, forcing, courant_rows, courant_cols, diffusion)

    mine = lax.all_to_all(messages, ("chip", "space"), 0, 0, tiled=True)
    other = lax.ppermute(mine, "core", [(0, 1), (1, 0)])
    rows = spaces * ROWS
    answer = pl.pallas_call(
        chain_kernel,
        in_specs=[SMEM, VMEM, VMEM],
        out_specs=VMEM,
        out_shape=shaped(chips * spaces, 24, LANES),
        scratch_shapes=[
            pltpu.VMEM((5, rows, LANES), F32),
            pltpu.VMEM((rows + 16, LANES), F32),
            pltpu.VMEM((rows + 16, LANES), F32),
        ],
        compiler_params=params(20),
        name="chain",
    )(flag, mine, other)
    returned = lax.all_to_all(answer, ("chip", "space"), 0, 0, tiled=True)
    return pl.pallas_call(
        final_kernel,
        in_specs=[VMEM] * 6,
        out_specs=VMEM,
        out_shape=shaped(4, ROWS, columns),
        scratch_shapes=[field, field, field, field, pltpu.VMEM((tiles, 8, LANES), F32)],
        compiler_params=params(20),
        name="final",
    )(start, coef, rims, forcing, ends, returned)


def solution(mesh):
    cores = 2
    devices = mesh.devices
    grid = Mesh(
        devices.reshape(devices.shape[0] // cores, cores, devices.shape[1]), ("chip", "core", "space")
    )
    time_rows = P(("chip", "core"), "space", None)
    rows = P("space", None)
    return jax.shard_map(
        on_device,
        mesh=grid,
        in_specs=(time_rows, time_rows, rows, rows, rows, rows),
        out_specs=time_rows,
        check_vma=False,
    )
```

```python
import jax
import jax.numpy as jnp
from jax import lax
from jax.experimental import pallas as pl
from jax.experimental.pallas import tpu as pltpu
from jax.sharding import Mesh, PartitionSpec as P

ROWS = 32
LANES = 128
HALO = 32
VMEM = pl.BlockSpec(memory_space=pltpu.VMEM)
SMEM = pl.BlockSpec(memory_space=pltpu.SMEM)
F32 = jnp.float32
ANY = pl.BlockSpec(memory_space=pl.ANY)
G1, G2, G3, PART, A1, B1, D1, INWARD = range(8)
START1, START2, STEP1, STEP2 = range(4)


def params(mib):
    return pltpu.CompilerParams(vmem_limit_bytes=mib * 1024 * 1024)


def iota(dim):
    return lax.broadcasted_iota(jnp.int32, (8, LANES), dim)


def cols(j):
    return slice(LANES * j, LANES * (j + 1))


def tile(r, first=0):
    return slice(first + 8 * r, first + 8 * r + 8)


def rates(a, b, d):
    a_pos, a_neg = jnp.maximum(a, 0.0), jnp.minimum(a, 0.0)
    b_pos, b_neg = jnp.maximum(b, 0.0), jnp.minimum(b, 0.0)
    own = 1.0 - (a_pos - a_neg) - (b_pos - b_neg) - 4.0 * d
    return own, d + a_pos, d - a_neg, d + b_pos, d - b_neg


def put(ref, j, r, value):
    ref[j, tile(r, 8), :] = value
    if r == 4:
        ref[j, 0:8, :] = value


def sweep(ref, coef, rows, use):
    tiles = ref.shape[0]
    lane = iota(1)
    for r in rows:
        at = 8 + 8 * r
        mids, rights, lefts = {}, {}, {}

        def load(j):
            j %= tiles
            if j not in mids:
                mids[j] = ref[j, at : at + 8, :]
                rights[j] = pltpu.roll(mids[j], 1, 1)
                lefts[j] = pltpu.roll(mids[j], LANES - 1, 1)

        for j in range(tiles):
            for i in (j - 1, j, j + 1):
                load(i)
            mid = mids[j]
            up = ref[j, at - 1 : at + 7, :]
            low = ref[j, at + 1 : at + 9, :] if r < 4 else ref[j, 1:9, :]
            left = jnp.where(lane == 0, rights[(j - 1) % tiles], rights[j])
            right = jnp.where(lane == LANES - 1, lefts[(j + 1) % tiles], lefts[j])
            total = coef[0, j, tile(r), :] * mid + coef[1, j, tile(r), :] * up
            total += coef[2, j, tile(r), :] * low + coef[3, j, tile(r), :] * left
            use(j, r, total + coef[4, j, tile(r), :] * right, mid)


def last_kernel(guess, last, sem):
    copy = pltpu.make_async_copy(guess.at[3], last, sem)
    copy.start()
    copy.wait()


class Tiles:
    def __init__(self, get):
        self.get, self.seen = get, {}

    def __getitem__(self, j):
        if j not in self.seen:
            self.seen[j] = self.get(j)
        return self.seen[j]


def rim_kernel(flag, guess, initial, a, b, d, forcing, rim_one, rim_two, start_one, start_two,
               va, vi, vg, vc, coef, field, part, after, sems):
    rows, columns = a.shape
    tiles = columns // LANES
    sub, lane = iota(0), iota(1)
    copies = []
    for side in range(2):
        at = pl.ds(0 if side == 0 else rows - 8, 8)
        moves = [(x.at[at, :], vc.at[i, side]) for i, x in enumerate((a, b, d))]
        moves += [(forcing.at[i, at, :], vg.at[i, side]) for i in range(3)]
        moves += [(guess.at[3, at, :], va.at[side]), (initial.at[at, :], vi.at[side])]
        for source, target in moves:
            copies.append(pltpu.make_async_copy(source, target, sems.at[len(copies)]))
    for copy in copies:
        copy.start()
    for copy in copies:
        copy.wait()
    at_end, even = flag[2] == 1, flag[4] == 0
    top = sub < 4

    def both(ref, j):
        return jnp.where(top, ref[0, :, cols(j)], ref[1, :, cols(j)])

    def outward(x):
        return jnp.where(top, pltpu.roll(x, 7, 0), pltpu.roll(x, 1, 0))

    def inward(x):
        return jnp.where(top, pltpu.roll(x, 1, 0), pltpu.roll(x, 7, 0))

    def row(x, side, place, to):
        at = place - 1 if side == 0 else 8 - place
        return pltpu.roll(x, (to - at) % 8, 0)

    OWN, OUT, IN, LEFT, RIGHT = range(5)

    def open_step(values, j):
        x, y, z = (values[i % tiles] for i in (j - 1, j, j + 1))
        left = pltpu.roll(jnp.where(lane == LANES - 1, x, y), 1, 1)
        right = pltpu.roll(jnp.where(lane == 0, z, y), LANES - 1, 1)
        total = coef[OWN, j] * y + coef[OUT, j] * outward(y)
        return total + (coef[LEFT, j] * left + coef[RIGHT, j] * right)

    for j in range(tiles):
        own, upper, lower, left, right = rates(*(both(vc.at[n], j) for n in range(3)))
        coef[OWN, j], coef[LEFT, j], coef[RIGHT, j] = own, left, right
        coef[OUT, j], coef[IN, j] = jnp.where(top, lower, upper), jnp.where(top, upper, lower)
        field[j] = jnp.where(at_end, both(vi, j), both(va, j))
    values = Tiles(lambda j: field[j])
    for j in range(tiles):
        part[j] = open_step(values, j)
        after[j] = part[j] + coef[IN, j] * inward(values[j])
    forced, stepped = Tiles(lambda j: both(vg.at[0], j)), Tiles(lambda j: after[j])
    for j in range(tiles):
        g1, g2, g3 = forced[j], both(vg.at[1], j), both(vg.at[2], j)
        items = [(G1, g1, 1), (G2, g2 + coef[OUT, j] * outward(g1), 1), (G3, g3, 1), (PART, open_step(forced, j) + g2, 2)]
        items += [(A1 + i, both(vc.at[i], j), 1) for i in range(3)]
        items += [(INWARD, coef[IN, j], 2)]
        values, second = field[j], open_step(stepped, j)
        begins = [(START1, values, 1), (START2, values, 2), (STEP1, part[j], 2), (STEP2, second, 2)]
        rims, starts = [], []
        for side in range(2):
            for found, made in ((items, rims), (begins, starts)):
                total = None
                for to, value, place in found:
                    value = row(value, side, place, to)
                    total = value if total is None else jnp.where(sub == to, value, total)
                made.append(total)
        rim_one[j] = jnp.where(even, rims[1], rims[0])
        rim_two[j] = jnp.where(even, rims[0], rims[1])
        start_one[j] = jnp.where(even, starts[1], starts[0])[0:4]
        start_two[j] = jnp.where(even, starts[0], starts[1])[0:4]


def residual_kernel(flag, before, initial, start_one, start_two, rim_one, rim_two, guess, forcing, a, b, d,
                    messages, ends, coef, two, three, four, rims, one, res, edge):
    tiles = a.shape[1] // LANES
    lane, sub = iota(1), iota(0)
    first, even = flag[0] == 1, flag[4] == 0
    turn = flag[3]
    zero = jnp.zeros((8, LANES), F32)
    for j in range(tiles):
        edge[0, j, 0:4, :] = jnp.where(even, start_one[j], start_two[j])
        edge[1, j, 0:4, :] = jnp.where(even, start_two[j], start_one[j])
    for j in range(tiles):
        low, up = jnp.where(even, rim_one[j], rim_two[j]), jnp.where(even, rim_two[j], rim_one[j])
        start_low, start_up = edge[0, j], edge[1, j]

        def border(under, over, item, place=1, rest=zero):
            under = pltpu.roll(under, (place - 1 - item) % 8, 0)
            over = pltpu.roll(over, (8 - place - item) % 8, 0)
            return jnp.where(sub == place - 1, under, jnp.where(sub == 8 - place, over, rest))

        for r in range(4):
            values = a[tile(r), cols(j)], b[tile(r), cols(j)], d[tile(r), cols(j)]
            put(one, j, r, jnp.where(first, initial[tile(r), cols(j)], before[tile(r), cols(j)]))
            for i, value in enumerate(rates(*values)):
                coef[i, j, tile(r), :] = value
        start = border(start_low, start_up, START1)
        put(one, j, 4, border(start_low, start_up, START2, 2, start))
        own, upper, lower, left, right = rates(*(border(low, up, item) for item in (A1, B1, D1)))
        own = jnp.where((sub == 0) | (sub == 7), own, 0.0)
        upper = jnp.where(sub == 1, pltpu.roll(low, (1 - INWARD) % 8, 0), upper)
        lower = jnp.where(sub == 6, pltpu.roll(up, (6 - INWARD) % 8, 0), lower)
        for i, value in enumerate((own, upper, lower, left, right)):
            coef[i, j, tile(4), :] = value
        rims[0, j] = border(start_low, start_up, STEP1, 2, border(low, up, G1))
        rims[1, j] = border(low, up, G2) + border(start_low, start_up, STEP2, 2) + border(low, up, PART, 2)
        rims[2, j] = border(low, up, G3)

    for inner, (source, target) in enumerate([(one, two), (two, three), (three, four)]):

        def fine(j, r, value, _, inner=inner, target=target):
            put(target, j, r, value + (forcing[inner, tile(r), cols(j)] if r < 4 else rims[inner, j]))

        sweep(source, coef, range(5), fine)

    def last(j, r, value, _):
        value = value + forcing[3, tile(r), cols(j)]
        ends[j, tile(r), :] = value
        res[j, tile(r), :] = value - guess[tile(r), cols(j)]

    sweep(four, coef, range(4), last)

    for r in range(4):
        for j in range(tiles):
            x, y, z = (res[i % tiles, tile(r), :] for i in (j - 1, j, j + 1))
            messages[2 * j, tile(r), :] = pltpu.roll(jnp.where(lane >= LANES - HALO, x, y), HALO, 1)
            messages[2 * j + 1, tile(r), :] = pltpu.roll(jnp.where(lane < HALO, z, y), LANES - HALO, 1)

    which, at = lax.div(turn, 4), pl.ds(pl.multiple_of(8 * lax.rem(turn, 4), 8), 8)
    for j in range(tiles):
        x, y, z = (
            jnp.where(which == 0, a[at, cols(i % tiles)], jnp.where(which == 1, b[at, cols(i % tiles)], d[at, cols(i % tiles)]))
            for i in (j - 1, j, j + 1)
        )
        messages[2 * j, tile(4), :] = pltpu.roll(jnp.where(lane >= LANES - HALO, x, y), HALO, 1)
        messages[2 * j + 1, tile(4), :] = pltpu.roll(jnp.where(lane < HALO, z, y), LANES - HALO, 1)


def chain_kernel(flag, mine, other, messages, coef, one, two):
    pairs = spaces = 8
    rows = spaces * ROWS
    blocks = rows // 8
    lane, sub = iota(1), iota(0)
    zero = jnp.zeros((8, LANES), F32)
    for ref in (one, two):
        ref[0:8, :] = zero
        ref[rows + 8 : rows + 16, :] = zero

    def step(source, t):
        at = 8 * t + 8
        mid = source[at : at + 8, :]
        total = coef[0, tile(t), :] * mid + coef[1, tile(t), :] * source[at - 1 : at + 7, :]
        total += coef[2, tile(t), :] * source[at + 1 : at + 9, :]
        total += coef[3, tile(t), :] * pltpu.roll(mid, 1, 1)
        return total + coef[4, tile(t), :] * pltpu.roll(mid, LANES - 1, 1)

    def emit(pair):
        for s in range(spaces):
            at = 8 + ROWS * s
            tiles = [one[tile(r, at), :] for r in range(4)]
            under, over = slice(at + ROWS, at + ROWS + 8), slice(at - 8, at)
            low_step = pltpu.roll(0.5 * (two[under, :] + one[under, :]), 1, 0)
            up_step = pltpu.roll(0.5 * (two[over, :] + one[over, :]), 7, 0)
            rim = jnp.where(sub < 2, one[under, :], one[over, :])
            rim = jnp.where(sub == 2, low_step, jnp.where(sub == 5, up_step, rim))
            low = [pltpu.roll(x, LANES - HALO, 1) for x in tiles[:3]]
            high = [pltpu.roll(x, HALO, 1) for x in (tiles[3], rim)]
            where = pair * spaces + s
            messages[where, 0:8, :] = jnp.where(lane < 64, low[0], high[0])
            messages[where, 8:16, :] = jnp.where(lane < 64, low[1], high[1])
            messages[where, 16:24, :] = low[2]

    def half():
        for t in range(blocks):
            two[tile(t, 8), :] = step(one, t)

    def run(even):
        sources = (mine, other) if even else (other, mine)

        def arrived(pair, odd, t):
            return sources[int(odd)][pair * spaces + t // 4, tile(t % 4), :]

        def rest(pair, odd):
            for t in range(blocks):
                one[tile(t, 8), :] = step(two, t) + arrived(pair, odd, t)

        for s in range(spaces):
            for r in range(4):
                a, b, d = (sources[r % 2][(4 * i + r) // 2 * spaces + s, tile(4), :] for i in range(3))
                own, up, low, left, right = rates(a, b, d)
                at = tile(r, s * ROWS)
                coef[0, at, :] = 2.0 * own - 1.0
                for i, value in enumerate((up, low, left, right)):
                    coef[i + 1, at, :] = 2.0 * value
        for t in range(blocks):
            one[tile(t, 8), :] = arrived(0, False, t)
        if even:
            for s in range(spaces):
                messages[s] = jnp.zeros((24, LANES), F32)

        def turn(pair, _):
            half()
            if not even:
                emit(pair)
            rest(pair, True)
            half()
            if even:
                emit(pair + 1)
            rest(pair + 1, False)
            return 0

        lax.fori_loop(0, pairs - 1, turn, 0)
        if not even:
            half()
            emit(pairs - 1)

    pl.when(flag[1] == 0)(lambda: run(True))
    pl.when(flag[1] != 0)(lambda: run(False))


def final_kernel(coef, first, second, third, ends, returned, states, err, one, two, extra, out, sems):
    tiles = first.shape[0]
    lane, sub = iota(1), iota(0)
    copies = [pltpu.make_async_copy(out.at[i], states.at[i], sems.at[i]) for i in range(4)]
    for j in range(tiles):
        for r in range(5):
            x, y = returned[2 * j, tile(r % 3), :], returned[2 * j + 1, tile(r % 3), :]
            if r < 3:
                error = jnp.where(lane < 64, x, pltpu.roll(y, 64, 1))
            else:
                error = jnp.where(lane < 64, pltpu.roll(x, 64, 1), y)
            put(err, j, r, error)
        after, behind = pltpu.roll(error, 7, 0), pltpu.roll(error, 1, 0)
        under = after - coef[1, j, tile(4), :] * behind
        over = behind - coef[2, j, tile(4), :] * after
        extra[j] = jnp.where(sub == 1, under, jnp.where(sub == 6, over, 0.0))

    def step_one(j, r, value, _):
        if r < 4:
            out[0, tile(r), cols(j)] = first[j, tile(r, 8), :] + value
        put(one, j, r, value if r < 4 else value + extra[j])

    def step_two(j, r, value, before):
        if r < 4:
            out[1, tile(r), cols(j)] = second[j, tile(r, 8), :] + value
            out[3, tile(r), cols(j)] = ends[j, tile(r), :] + (4.0 * (value - before) + err[j, tile(r, 8), :])
        put(two, j, r, value)

    def step_three(j, r, value, _):
        out[2, tile(r), cols(j)] = third[j, tile(r, 8), :] + value

    sweep(err, coef, range(5), step_one)
    copies[0].start()
    sweep(one, coef, range(5), step_two)
    copies[1].start()
    copies[3].start()
    sweep(two, coef, range(4), step_three)
    copies[2].start()
    for copy in copies:
        copy.wait()


def on_device(guess, forcing, initial, courant_rows, courant_cols, diffusion):
    chips, cores, spaces = (lax.axis_size(n) for n in ("chip", "core", "space"))
    owners = chips * cores
    columns = initial.shape[1]
    tiles = columns // LANES
    everything = ("chip", "core", "space")
    chip, core = lax.axis_index("chip"), lax.axis_index("core")
    turn = chip * cores + core
    flag = jnp.stack([turn == 0, core, turn == owners - 1, turn, lax.axis_index("space") % 2]).astype(jnp.int32)

    def shaped(*shape):
        return jax.ShapeDtypeStruct(shape, F32)

    last = pl.pallas_call(
        last_kernel,
        in_specs=[ANY],
        out_specs=VMEM,
        out_shape=shaped(ROWS, columns),
        scratch_shapes=[pltpu.SemaphoreType.DMA],
        compiler_params=params(52),
        name="last",
    )(guess)
    before = lax.ppermute(last, ("chip", "core"), [(i, i + 1) for i in range(owners - 1)])
    small = pltpu.VMEM((tiles, 8, LANES), F32)
    edge_rows = pltpu.VMEM((2, 8, columns), F32)
    rim_one, rim_two, start_one, start_two = pl.pallas_call(
        rim_kernel,
        in_specs=[SMEM] + [ANY] * 6,
        out_specs=[VMEM] * 4,
        out_shape=[shaped(tiles, 8, LANES), shaped(tiles, 8, LANES), shaped(tiles, 4, LANES), shaped(tiles, 4, LANES)],
        scratch_shapes=[
            edge_rows,
            edge_rows,
            pltpu.VMEM((3, 2, 8, columns), F32),
            pltpu.VMEM((3, 2, 8, columns), F32),
            pltpu.VMEM((5, tiles, 8, LANES), F32),
            small,
            small,
            small,
            pltpu.SemaphoreType.DMA((16,)),
        ],
        compiler_params=params(52),
        name="rim",
    )(flag, guess, initial, courant_rows, courant_cols, diffusion, forcing)

    def exchanged(value, by_turn, first):
        pairs = []
        for k in range(owners):
            for s in range(spaces):
                partner = s + 1 if (s % 2 == 0) == first else s - 1
                if 0 <= partner < spaces:
                    pairs.append((k * spaces + s, (k + by_turn) % owners * spaces + partner))
        return lax.ppermute(value, everything, pairs)

    rim_one, rim_two = exchanged(rim_one, 0, True), exchanged(rim_two, 0, False)
    start_one, start_two = exchanged(start_one, 1, True), exchanged(start_two, 1, False)

    field = pltpu.VMEM((tiles, 48, LANES), F32)
    tall = shaped(tiles, 48, LANES)
    messages, ends, coef, *fields = pl.pallas_call(
        residual_kernel,
        in_specs=[SMEM] + [VMEM] * 11,
        out_specs=[VMEM] * 6,
        out_shape=[shaped(2 * tiles, 40, LANES), shaped(tiles, ROWS, LANES), shaped(5, tiles, 40, LANES), tall, tall, tall],
        scratch_shapes=[
            pltpu.VMEM((3, tiles, 8, LANES), F32),
            field,
            pltpu.VMEM((tiles, ROWS, LANES), F32),
            pltpu.VMEM((2, tiles, 8, LANES), F32),
        ],
        compiler_params=params(20),
        name="residual",
    )(flag, before, initial, start_one, start_two, rim_one, rim_two, last, forcing, courant_rows, courant_cols, diffusion)

    mine = lax.all_to_all(messages, ("chip", "space"), 0, 0, tiled=True)
    other = lax.ppermute(mine, "core", [(0, 1), (1, 0)])
    rows = spaces * ROWS
    answer = pl.pallas_call(
        chain_kernel,
        in_specs=[SMEM, VMEM, VMEM],
        out_specs=VMEM,
        out_shape=shaped(chips * spaces, 24, LANES),
        scratch_shapes=[
            pltpu.VMEM((5, rows, LANES), F32),
            pltpu.VMEM((rows + 16, LANES), F32),
            pltpu.VMEM((rows + 16, LANES), F32),
        ],
        compiler_params=params(20),
        name="chain",
    )(flag, mine, other)
    returned = lax.all_to_all(answer, ("chip", "space"), 0, 0, tiled=True)
    return pl.pallas_call(
        final_kernel,
        in_specs=[VMEM] * 6,
        out_specs=ANY,
        out_shape=shaped(4, ROWS, columns),
        scratch_shapes=[field, field, field, small, pltpu.VMEM((4, ROWS, columns), F32), pltpu.SemaphoreType.DMA((4,))],
        compiler_params=params(20),
        name="final",
    )(coef, *fields, ends, returned)


def solution(mesh):
    cores = 2
    devices = mesh.devices
    grid = Mesh(
        devices.reshape(devices.shape[0] // cores, cores, devices.shape[1]), ("chip", "core", "space")
    )
    time_rows = P(("chip", "core"), "space", None)
    rows = P("space", None)
    return jax.shard_map(
        on_device,
        mesh=grid,
        in_specs=(time_rows, time_rows, rows, rows, rows, rows),
        out_specs=time_rows,
        check_vma=False,
    )
```

```python
import jax
import jax.numpy as jnp
from jax import lax
from jax.experimental import pallas as pl
from jax.experimental.pallas import tpu as pltpu
from jax.sharding import Mesh, PartitionSpec as P

ROWS = 32
LANES = 128
HALO = 32
VMEM = pl.BlockSpec(memory_space=pltpu.VMEM)
SMEM = pl.BlockSpec(memory_space=pltpu.SMEM)
F32 = jnp.float32
ANY = pl.BlockSpec(memory_space=pl.ANY)
G1, G2, G3, PART, A1, B1, D1, INWARD = range(8)
START1, START2, STEP1, STEP2 = range(4)


def params(mib):
    return pltpu.CompilerParams(vmem_limit_bytes=mib * 1024 * 1024)


def iota(dim):
    return lax.broadcasted_iota(jnp.int32, (8, LANES), dim)


def cols(j):
    return slice(LANES * j, LANES * (j + 1))


def tile(r, first=0):
    return slice(first + 8 * r, first + 8 * r + 8)


def rates(a, b, d):
    a_pos, a_neg = jnp.maximum(a, 0.0), jnp.minimum(a, 0.0)
    b_pos, b_neg = jnp.maximum(b, 0.0), jnp.minimum(b, 0.0)
    own = 1.0 - (a_pos - a_neg) - (b_pos - b_neg) - 4.0 * d
    return own, d + a_pos, d - a_neg, d + b_pos, d - b_neg


def put(ref, j, r, value):
    ref[j, tile(r, 8), :] = value
    if r == 4:
        ref[j, 0:8, :] = value


def sweep(ref, coef, rows, use):
    tiles = ref.shape[0]
    lane = iota(1)
    for r in rows:
        at = 8 + 8 * r
        mids, rights, lefts = {}, {}, {}

        def load(j):
            j %= tiles
            if j not in mids:
                mids[j] = ref[j, at : at + 8, :]
                rights[j] = pltpu.roll(mids[j], 1, 1)
                lefts[j] = pltpu.roll(mids[j], LANES - 1, 1)

        for j in range(tiles):
            for i in (j - 1, j, j + 1):
                load(i)
            mid = mids[j]
            up = ref[j, at - 1 : at + 7, :]
            low = ref[j, at + 1 : at + 9, :] if r < 4 else ref[j, 1:9, :]
            left = jnp.where(lane == 0, rights[(j - 1) % tiles], rights[j])
            right = jnp.where(lane == LANES - 1, lefts[(j + 1) % tiles], lefts[j])
            total = coef[0, j, tile(r), :] * mid + coef[1, j, tile(r), :] * up
            total += coef[2, j, tile(r), :] * low + coef[3, j, tile(r), :] * left
            use(j, r, total + coef[4, j, tile(r), :] * right, mid)


def last_kernel(guess, last, sem):
    copy = pltpu.make_async_copy(guess.at[3], last, sem)
    copy.start()
    copy.wait()


class Tiles:
    def __init__(self, get):
        self.get, self.seen = get, {}

    def __getitem__(self, j):
        if j not in self.seen:
            self.seen[j] = self.get(j)
        return self.seen[j]


def rim_kernel(flag, guess, initial, a, b, d, forcing, rim_one, rim_two, start_one, start_two,
               va, vi, vg, vc, coef, field, part, after, sems):
    rows, columns = a.shape
    tiles = columns // LANES
    sub, lane = iota(0), iota(1)
    copies = []
    for side in range(2):
        at = pl.ds(0 if side == 0 else rows - 8, 8)
        moves = [(x.at[at, :], vc.at[i, side]) for i, x in enumerate((a, b, d))]
        moves += [(forcing.at[i, at, :], vg.at[i, side]) for i in range(3)]
        moves += [(guess.at[3, at, :], va.at[side]), (initial.at[at, :], vi.at[side])]
        for source, target in moves:
            copies.append(pltpu.make_async_copy(source, target, sems.at[len(copies)]))
    for copy in copies:
        copy.start()
    for copy in copies:
        copy.wait()
    at_end, even = flag[2] == 1, flag[4] == 0
    top = sub < 4

    def both(ref, j):
        return jnp.where(top, ref[0, :, cols(j)], ref[1, :, cols(j)])

    def outward(x):
        return jnp.where(top, pltpu.roll(x, 7, 0), pltpu.roll(x, 1, 0))

    def inward(x):
        return jnp.where(top, pltpu.roll(x, 1, 0), pltpu.roll(x, 7, 0))

    def row(x, side, place, to):
        at = place - 1 if side == 0 else 8 - place
        return pltpu.roll(x, (to - at) % 8, 0)

    OWN, OUT, IN, LEFT, RIGHT = range(5)

    def open_step(values, j):
        x, y, z = (values[i % tiles] for i in (j - 1, j, j + 1))
        left = pltpu.roll(jnp.where(lane == LANES - 1, x, y), 1, 1)
        right = pltpu.roll(jnp.where(lane == 0, z, y), LANES - 1, 1)
        total = coef[OWN, j] * y + coef[OUT, j] * outward(y)
        return total + (coef[LEFT, j] * left + coef[RIGHT, j] * right)

    for j in range(tiles):
        own, upper, lower, left, right = rates(*(both(vc.at[n], j) for n in range(3)))
        coef[OWN, j], coef[LEFT, j], coef[RIGHT, j] = own, left, right
        coef[OUT, j], coef[IN, j] = jnp.where(top, lower, upper), jnp.where(top, upper, lower)
        field[j] = jnp.where(at_end, both(vi, j), both(va, j))
    values = Tiles(lambda j: field[j])
    for j in range(tiles):
        part[j] = open_step(values, j)
        after[j] = part[j] + coef[IN, j] * inward(values[j])
    forced, stepped = Tiles(lambda j: both(vg.at[0], j)), Tiles(lambda j: after[j])
    for j in range(tiles):
        g1, g2, g3 = forced[j], both(vg.at[1], j), both(vg.at[2], j)
        items = [(G1, g1, 1), (G2, g2 + coef[OUT, j] * outward(g1), 1), (G3, g3, 1), (PART, open_step(forced, j) + g2, 2)]
        items += [(A1 + i, both(vc.at[i], j), 1) for i in range(3)]
        items += [(INWARD, coef[IN, j], 2)]
        values, second = field[j], open_step(stepped, j)
        begins = [(START1, values, 1), (START2, values, 2), (STEP1, part[j], 2), (STEP2, second, 2)]
        rims, starts = [], []
        for side in range(2):
            for found, made in ((items, rims), (begins, starts)):
                total = None
                for to, value, place in found:
                    value = row(value, side, place, to)
                    total = value if total is None else jnp.where(sub == to, value, total)
                made.append(total)
        rim_one[j] = jnp.where(even, rims[1], rims[0])
        rim_two[j] = jnp.where(even, rims[0], rims[1])
        start_one[j] = jnp.where(even, starts[1], starts[0])[0:4]
        start_two[j] = jnp.where(even, starts[0], starts[1])[0:4]


def border(sub, under, over, item, place=1, rest=0.0):
    under = pltpu.roll(under, (place - 1 - item) % 8, 0)
    over = pltpu.roll(over, (8 - place - item) % 8, 0)
    return jnp.where(sub == place - 1, under, jnp.where(sub == 8 - place, over, rest))


def prepare_kernel(flag, rim_one, rim_two, a, b, d, coef, rims, packed):
    tiles = a.shape[1] // LANES
    lane, sub = iota(1), iota(0)
    even, turn = flag[4] == 0, flag[3]
    for j in range(tiles):
        low, up = jnp.where(even, rim_one[j], rim_two[j]), jnp.where(even, rim_two[j], rim_one[j])
        for r in range(4):
            values = a[tile(r), cols(j)], b[tile(r), cols(j)], d[tile(r), cols(j)]
            for i, value in enumerate(rates(*values)):
                coef[i, j, tile(r), :] = value
        own, upper, lower, left, right = rates(*(border(sub, low, up, item) for item in (A1, B1, D1)))
        own = jnp.where((sub == 0) | (sub == 7), own, 0.0)
        upper = jnp.where(sub == 1, pltpu.roll(low, (1 - INWARD) % 8, 0), upper)
        lower = jnp.where(sub == 6, pltpu.roll(up, (6 - INWARD) % 8, 0), lower)
        for i, value in enumerate((own, upper, lower, left, right)):
            coef[i, j, tile(4), :] = value
        rims[0, j] = border(sub, low, up, G1)
        rims[1, j] = border(sub, low, up, PART, 2, border(sub, low, up, G2))
        rims[2, j] = border(sub, low, up, G3)
    which, at = lax.div(turn, 4), pl.ds(pl.multiple_of(8 * lax.rem(turn, 4), 8), 8)
    chosen = Tiles(lambda j: jnp.where(which == 0, a[at, cols(j)], jnp.where(which == 1, b[at, cols(j)], d[at, cols(j)])))
    for j in range(tiles):
        x, y, z = (chosen[i % tiles] for i in (j - 1, j, j + 1))
        packed[2 * j] = pltpu.roll(jnp.where(lane >= LANES - HALO, x, y), HALO, 1)
        packed[2 * j + 1] = pltpu.roll(jnp.where(lane < HALO, z, y), LANES - HALO, 1)


def residual_kernel(flag, before, initial, start_one, start_two, guess, forcing, coef, rims, packed,
                    messages, ends, two, three, four, one, res, edge, begin):
    tiles = guess.shape[1] // LANES
    lane, sub = iota(1), iota(0)
    first, even = flag[0] == 1, flag[4] == 0
    for j in range(tiles):
        edge[0, j, 0:4, :] = jnp.where(even, start_one[j], start_two[j])
        edge[1, j, 0:4, :] = jnp.where(even, start_two[j], start_one[j])
        for i in (2 * j, 2 * j + 1):
            messages[i, tile(4), :] = packed[i]
    for j in range(tiles):
        low, up = edge[0, j], edge[1, j]
        for r in range(4):
            put(one, j, r, jnp.where(first, initial[tile(r), cols(j)], before[tile(r), cols(j)]))
        put(one, j, 4, border(sub, low, up, START2, 2, border(sub, low, up, START1)))
        begin[0, j] = border(sub, low, up, STEP1, 2, rims[0, j])
        begin[1, j] = rims[1, j] + border(sub, low, up, STEP2, 2)
        begin[2, j] = rims[2, j]

    for inner, (source, target) in enumerate([(one, two), (two, three), (three, four)]):

        def fine(j, r, value, _, inner=inner, target=target):
            put(target, j, r, value + (forcing[inner, tile(r), cols(j)] if r < 4 else begin[inner, j]))

        sweep(source, coef, range(5), fine)

    def last(j, r, value, _):
        value = value + forcing[3, tile(r), cols(j)]
        ends[j, tile(r), :] = value
        res[j, tile(r), :] = value - guess[tile(r), cols(j)]

    sweep(four, coef, range(4), last)

    for r in range(4):
        for j in range(tiles):
            x, y, z = (res[i % tiles, tile(r), :] for i in (j - 1, j, j + 1))
            messages[2 * j, tile(r), :] = pltpu.roll(jnp.where(lane >= LANES - HALO, x, y), HALO, 1)
            messages[2 * j + 1, tile(r), :] = pltpu.roll(jnp.where(lane < HALO, z, y), LANES - HALO, 1)


def chain_kernel(flag, mine, other, messages, coef, one, two):
    pairs = spaces = 8
    rows = spaces * ROWS
    blocks = rows // 8
    lane, sub = iota(1), iota(0)
    zero = jnp.zeros((8, LANES), F32)
    for ref in (one, two):
        ref[0:8, :] = zero
        ref[rows + 8 : rows + 16, :] = zero

    def step(source, t):
        at = 8 * t + 8
        mid = source[at : at + 8, :]
        total = coef[0, tile(t), :] * mid + coef[1, tile(t), :] * source[at - 1 : at + 7, :]
        total += coef[2, tile(t), :] * source[at + 1 : at + 9, :]
        total += coef[3, tile(t), :] * pltpu.roll(mid, 1, 1)
        return total + coef[4, tile(t), :] * pltpu.roll(mid, LANES - 1, 1)

    def emit(pair):
        for s in range(spaces):
            at = 8 + ROWS * s
            tiles = [one[tile(r, at), :] for r in range(4)]
            under, over = slice(at + ROWS, at + ROWS + 8), slice(at - 8, at)
            low_step = pltpu.roll(0.5 * (two[under, :] + one[under, :]), 1, 0)
            up_step = pltpu.roll(0.5 * (two[over, :] + one[over, :]), 7, 0)
            rim = jnp.where(sub < 2, one[under, :], one[over, :])
            rim = jnp.where(sub == 2, low_step, jnp.where(sub == 5, up_step, rim))
            low = [pltpu.roll(x, LANES - HALO, 1) for x in tiles[:3]]
            high = [pltpu.roll(x, HALO, 1) for x in (tiles[3], rim)]
            where = pair * spaces + s
            messages[where, 0:8, :] = jnp.where(lane < 64, low[0], high[0])
            messages[where, 8:16, :] = jnp.where(lane < 64, low[1], high[1])
            messages[where, 16:24, :] = low[2]

    def half():
        for t in range(blocks):
            two[tile(t, 8), :] = step(one, t)

    def run(even):
        sources = (mine, other) if even else (other, mine)

        def arrived(pair, odd, t):
            return sources[int(odd)][pair * spaces + t // 4, tile(t % 4), :]

        def rest(pair, odd):
            for t in range(blocks):
                one[tile(t, 8), :] = step(two, t) + arrived(pair, odd, t)

        for s in range(spaces):
            for r in range(4):
                a, b, d = (sources[r % 2][(4 * i + r) // 2 * spaces + s, tile(4), :] for i in range(3))
                own, up, low, left, right = rates(a, b, d)
                at = tile(r, s * ROWS)
                coef[0, at, :] = 2.0 * own - 1.0
                for i, value in enumerate((up, low, left, right)):
                    coef[i + 1, at, :] = 2.0 * value
        for t in range(blocks):
            one[tile(t, 8), :] = arrived(0, False, t)
        if even:
            for s in range(spaces):
                messages[s] = jnp.zeros((24, LANES), F32)

        def turn(pair, _):
            half()
            if not even:
                emit(pair)
            rest(pair, True)
            half()
            if even:
                emit(pair + 1)
            rest(pair + 1, False)
            return 0

        lax.fori_loop(0, pairs - 1, turn, 0)
        if not even:
            half()
            emit(pairs - 1)

    pl.when(flag[1] == 0)(lambda: run(True))
    pl.when(flag[1] != 0)(lambda: run(False))


def final_kernel(coef, first, second, third, ends, returned, states, err, one, two, extra, out, sems):
    tiles = first.shape[0]
    lane, sub = iota(1), iota(0)
    copies = [pltpu.make_async_copy(out.at[i], states.at[i], sems.at[i]) for i in range(4)]
    for j in range(tiles):
        for r in range(5):
            x, y = returned[2 * j, tile(r % 3), :], returned[2 * j + 1, tile(r % 3), :]
            if r < 3:
                error = jnp.where(lane < 64, x, pltpu.roll(y, 64, 1))
            else:
                error = jnp.where(lane < 64, pltpu.roll(x, 64, 1), y)
            put(err, j, r, error)
        after, behind = pltpu.roll(error, 7, 0), pltpu.roll(error, 1, 0)
        under = after - coef[1, j, tile(4), :] * behind
        over = behind - coef[2, j, tile(4), :] * after
        extra[j] = jnp.where(sub == 1, under, jnp.where(sub == 6, over, 0.0))

    def step_one(j, r, value, _):
        if r < 4:
            out[0, tile(r), cols(j)] = first[j, tile(r, 8), :] + value
        put(one, j, r, value if r < 4 else value + extra[j])

    def step_two(j, r, value, before):
        if r < 4:
            out[1, tile(r), cols(j)] = second[j, tile(r, 8), :] + value
            out[3, tile(r), cols(j)] = ends[j, tile(r), :] + (4.0 * (value - before) + err[j, tile(r, 8), :])
        put(two, j, r, value)

    def step_three(j, r, value, _):
        out[2, tile(r), cols(j)] = third[j, tile(r, 8), :] + value

    sweep(err, coef, range(5), step_one)
    copies[0].start()
    sweep(one, coef, range(5), step_two)
    copies[1].start()
    copies[3].start()
    sweep(two, coef, range(4), step_three)
    copies[2].start()
    for copy in copies:
        copy.wait()


def on_device(guess, forcing, initial, courant_rows, courant_cols, diffusion):
    chips, cores, spaces = (lax.axis_size(n) for n in ("chip", "core", "space"))
    owners = chips * cores
    columns = initial.shape[1]
    tiles = columns // LANES
    everything = ("chip", "core", "space")
    chip, core = lax.axis_index("chip"), lax.axis_index("core")
    turn = chip * cores + core
    flag = jnp.stack([turn == 0, core, turn == owners - 1, turn, lax.axis_index("space") % 2]).astype(jnp.int32)

    def shaped(*shape):
        return jax.ShapeDtypeStruct(shape, F32)

    last = pl.pallas_call(
        last_kernel,
        in_specs=[ANY],
        out_specs=VMEM,
        out_shape=shaped(ROWS, columns),
        scratch_shapes=[pltpu.SemaphoreType.DMA],
        compiler_params=params(52),
        name="last",
    )(guess)
    before = lax.ppermute(last, ("chip", "core"), [(i, i + 1) for i in range(owners - 1)])
    small = pltpu.VMEM((tiles, 8, LANES), F32)
    edge_rows = pltpu.VMEM((2, 8, columns), F32)
    rim_one, rim_two, start_one, start_two = pl.pallas_call(
        rim_kernel,
        in_specs=[SMEM] + [ANY] * 6,
        out_specs=[VMEM] * 4,
        out_shape=[shaped(tiles, 8, LANES), shaped(tiles, 8, LANES), shaped(tiles, 4, LANES), shaped(tiles, 4, LANES)],
        scratch_shapes=[
            edge_rows,
            edge_rows,
            pltpu.VMEM((3, 2, 8, columns), F32),
            pltpu.VMEM((3, 2, 8, columns), F32),
            pltpu.VMEM((5, tiles, 8, LANES), F32),
            small,
            small,
            small,
            pltpu.SemaphoreType.DMA((16,)),
        ],
        compiler_params=params(52),
        name="rim",
    )(flag, guess, initial, courant_rows, courant_cols, diffusion, forcing)

    def exchanged(value, by_turn, first):
        pairs = []
        for k in range(owners):
            for s in range(spaces):
                partner = s + 1 if (s % 2 == 0) == first else s - 1
                if 0 <= partner < spaces:
                    pairs.append((k * spaces + s, (k + by_turn) % owners * spaces + partner))
        return lax.ppermute(value, everything, pairs)

    rim_one, rim_two = exchanged(rim_one, 0, True), exchanged(rim_two, 0, False)
    start_one, start_two = exchanged(start_one, 1, True), exchanged(start_two, 1, False)

    field = pltpu.VMEM((tiles, 48, LANES), F32)
    tall = shaped(tiles, 48, LANES)
    coef, rims, packed = pl.pallas_call(
        prepare_kernel,
        in_specs=[SMEM] + [VMEM] * 5,
        out_specs=[VMEM] * 3,
        out_shape=[shaped(5, tiles, 40, LANES), shaped(3, tiles, 8, LANES), shaped(2 * tiles, 8, LANES)],
        compiler_params=params(20),
        name="prepare",
    )(flag, rim_one, rim_two, courant_rows, courant_cols, diffusion)
    messages, ends, *fields = pl.pallas_call(
        residual_kernel,
        in_specs=[SMEM] + [VMEM] * 9,
        out_specs=[VMEM] * 5,
        out_shape=[shaped(2 * tiles, 40, LANES), shaped(tiles, ROWS, LANES), tall, tall, tall],
        scratch_shapes=[
            field,
            pltpu.VMEM((tiles, ROWS, LANES), F32),
            pltpu.VMEM((2, tiles, 8, LANES), F32),
            pltpu.VMEM((3, tiles, 8, LANES), F32),
        ],
        compiler_params=params(20),
        name="residual",
    )(flag, before, initial, start_one, start_two, last, forcing, coef, rims, packed)

    mine = lax.all_to_all(messages, ("chip", "space"), 0, 0, tiled=True)
    other = lax.ppermute(mine, "core", [(0, 1), (1, 0)])
    rows = spaces * ROWS
    answer = pl.pallas_call(
        chain_kernel,
        in_specs=[SMEM, VMEM, VMEM],
        out_specs=VMEM,
        out_shape=shaped(chips * spaces, 24, LANES),
        scratch_shapes=[
            pltpu.VMEM((5, rows, LANES), F32),
            pltpu.VMEM((rows + 16, LANES), F32),
            pltpu.VMEM((rows + 16, LANES), F32),
        ],
        compiler_params=params(20),
        name="chain",
    )(flag, mine, other)
    returned = lax.all_to_all(answer, ("chip", "space"), 0, 0, tiled=True)
    return pl.pallas_call(
        final_kernel,
        in_specs=[VMEM] * 6,
        out_specs=ANY,
        out_shape=shaped(4, ROWS, columns),
        scratch_shapes=[field, field, field, small, pltpu.VMEM((4, ROWS, columns), F32), pltpu.SemaphoreType.DMA((4,))],
        compiler_params=params(20),
        name="final",
    )(coef, *fields, ends, returned)


def solution(mesh):
    cores = 2
    devices = mesh.devices
    grid = Mesh(
        devices.reshape(devices.shape[0] // cores, cores, devices.shape[1]), ("chip", "core", "space")
    )
    time_rows = P(("chip", "core"), "space", None)
    rows = P("space", None)
    return jax.shard_map(
        on_device,
        mesh=grid,
        in_specs=(time_rows, time_rows, rows, rows, rows, rows),
        out_specs=time_rows,
        check_vma=False,
    )
```

```python
import jax
import jax.numpy as jnp
from jax import lax
from jax.experimental import pallas as pl
from jax.experimental.pallas import tpu as pltpu
from jax.sharding import Mesh, PartitionSpec as P

ROWS = 32
LANES = 128
HALO = 32
VMEM = pl.BlockSpec(memory_space=pltpu.VMEM)
SMEM = pl.BlockSpec(memory_space=pltpu.SMEM)
F32 = jnp.float32
ANY = pl.BlockSpec(memory_space=pl.ANY)
G1, G2, G3, PART, A1, B1, D1, INWARD = range(8)
START1, START2, STEP1, STEP2 = range(4)


def params(mib):
    return pltpu.CompilerParams(vmem_limit_bytes=mib * 1024 * 1024)


def iota(dim):
    return lax.broadcasted_iota(jnp.int32, (8, LANES), dim)


def cols(j):
    return slice(LANES * j, LANES * (j + 1))


def tile(r, first=0):
    return slice(first + 8 * r, first + 8 * r + 8)


def rates(a, b, d):
    a_pos, a_neg = jnp.maximum(a, 0.0), jnp.minimum(a, 0.0)
    b_pos, b_neg = jnp.maximum(b, 0.0), jnp.minimum(b, 0.0)
    own = 1.0 - (a_pos - a_neg) - (b_pos - b_neg) - 4.0 * d
    return own, d + a_pos, d - a_neg, d + b_pos, d - b_neg


def put(ref, j, r, value):
    ref[j, tile(r, 8), :] = value
    if r == 4:
        ref[j, 0:8, :] = value


def sweep(ref, coef, rows, use):
    tiles = ref.shape[0]
    lane = iota(1)
    for r in rows:
        at = 8 + 8 * r
        mids, rights, lefts = {}, {}, {}

        def load(j):
            j %= tiles
            if j not in mids:
                mids[j] = ref[j, at : at + 8, :]
                rights[j] = pltpu.roll(mids[j], 1, 1)
                lefts[j] = pltpu.roll(mids[j], LANES - 1, 1)

        for j in range(tiles):
            for i in (j - 1, j, j + 1):
                load(i)
            mid = mids[j]
            up = ref[j, at - 1 : at + 7, :]
            low = ref[j, at + 1 : at + 9, :] if r < 4 else ref[j, 1:9, :]
            left = jnp.where(lane == 0, rights[(j - 1) % tiles], rights[j])
            right = jnp.where(lane == LANES - 1, lefts[(j + 1) % tiles], lefts[j])
            total = coef[0, j, tile(r), :] * mid + coef[1, j, tile(r), :] * up
            total += coef[2, j, tile(r), :] * low + coef[3, j, tile(r), :] * left
            use(j, r, total + coef[4, j, tile(r), :] * right, mid)


def last_kernel(guess, last, sem):
    copy = pltpu.make_async_copy(guess.at[3], last, sem)
    copy.start()
    copy.wait()


class Tiles:
    def __init__(self, get):
        self.get, self.seen = get, {}

    def __getitem__(self, j):
        if j not in self.seen:
            self.seen[j] = self.get(j)
        return self.seen[j]


def rim_kernel(flag, last, initial, a, b, d, forcing, rim_one, rim_two, start_one, start_two,
               vg, coef, field, part, after, sems):
    rows, columns = a.shape
    tiles = columns // LANES
    sub, lane = iota(0), iota(1)
    copies = []
    for side, at in enumerate((pl.ds(0, 8), pl.ds(rows - 8, 8))):
        for i in range(3):
            source, target = forcing.at[i, at, :], vg.at[i, pl.ds(8 * side, 8), :]
            copies.append(pltpu.make_async_copy(source, target, sems.at[len(copies)]))
    for copy in copies:
        copy.start()
    at_end, even = flag[2] == 1, flag[4] == 0
    top = sub < 4

    def both(ref, j):
        end = ref.shape[0]
        return jnp.where(top, ref[0:8, cols(j)], ref[end - 8 : end, cols(j)])

    def outward(x):
        return jnp.where(top, pltpu.roll(x, 7, 0), pltpu.roll(x, 1, 0))

    def inward(x):
        return jnp.where(top, pltpu.roll(x, 1, 0), pltpu.roll(x, 7, 0))

    def row(x, side, place, to):
        at = place - 1 if side == 0 else 8 - place
        return pltpu.roll(x, (to - at) % 8, 0)

    OWN, OUT, IN, LEFT, RIGHT = range(5)

    def open_step(values, j):
        x, y, z = (values[i % tiles] for i in (j - 1, j, j + 1))
        left = pltpu.roll(jnp.where(lane == LANES - 1, x, y), 1, 1)
        right = pltpu.roll(jnp.where(lane == 0, z, y), LANES - 1, 1)
        total = coef[OWN, j] * y + coef[OUT, j] * outward(y)
        return total + (coef[LEFT, j] * left + coef[RIGHT, j] * right)

    for j in range(tiles):
        own, upper, lower, left, right = rates(*(both(x, j) for x in (a, b, d)))
        coef[OWN, j], coef[LEFT, j], coef[RIGHT, j] = own, left, right
        coef[OUT, j], coef[IN, j] = jnp.where(top, lower, upper), jnp.where(top, upper, lower)
        field[j] = jnp.where(at_end, both(initial, j), both(last, j))
    values = Tiles(lambda j: field[j])
    for j in range(tiles):
        part[j] = open_step(values, j)
        after[j] = part[j] + coef[IN, j] * inward(values[j])
    for copy in copies:
        copy.wait()
    forced, stepped = Tiles(lambda j: both(vg.at[0], j)), Tiles(lambda j: after[j])
    for j in range(tiles):
        g1, g2, g3 = forced[j], both(vg.at[1], j), both(vg.at[2], j)
        items = [(G1, g1, 1), (G2, g2 + coef[OUT, j] * outward(g1), 1), (G3, g3, 1), (PART, open_step(forced, j) + g2, 2)]
        items += [(A1 + i, both(x, j), 1) for i, x in enumerate((a, b, d))]
        items += [(INWARD, coef[IN, j], 2)]
        values, second = field[j], open_step(stepped, j)
        begins = [(START1, values, 1), (START2, values, 2), (STEP1, part[j], 2), (STEP2, second, 2)]
        rims, starts = [], []
        for side in range(2):
            for found, made in ((items, rims), (begins, starts)):
                total = None
                for to, value, place in found:
                    value = row(value, side, place, to)
                    total = value if total is None else jnp.where(sub == to, value, total)
                made.append(total)
        rim_one[j] = jnp.where(even, rims[1], rims[0])
        rim_two[j] = jnp.where(even, rims[0], rims[1])
        start_one[j] = jnp.where(even, starts[1], starts[0])[0:4]
        start_two[j] = jnp.where(even, starts[0], starts[1])[0:4]


def border(sub, under, over, item, place=1, rest=0.0):
    under = pltpu.roll(under, (place - 1 - item) % 8, 0)
    over = pltpu.roll(over, (8 - place - item) % 8, 0)
    return jnp.where(sub == place - 1, under, jnp.where(sub == 8 - place, over, rest))


def prepare_kernel(flag, rim_one, rim_two, a, b, d, coef, rims, packed):
    tiles = a.shape[1] // LANES
    lane, sub = iota(1), iota(0)
    even, turn = flag[4] == 0, flag[3]
    for j in range(tiles):
        low, up = jnp.where(even, rim_one[j], rim_two[j]), jnp.where(even, rim_two[j], rim_one[j])
        for r in range(4):
            values = a[tile(r), cols(j)], b[tile(r), cols(j)], d[tile(r), cols(j)]
            for i, value in enumerate(rates(*values)):
                coef[i, j, tile(r), :] = value
        own, upper, lower, left, right = rates(*(border(sub, low, up, item) for item in (A1, B1, D1)))
        own = jnp.where((sub == 0) | (sub == 7), own, 0.0)
        upper = jnp.where(sub == 1, pltpu.roll(low, (1 - INWARD) % 8, 0), upper)
        lower = jnp.where(sub == 6, pltpu.roll(up, (6 - INWARD) % 8, 0), lower)
        for i, value in enumerate((own, upper, lower, left, right)):
            coef[i, j, tile(4), :] = value
        rims[0, j] = border(sub, low, up, G1)
        rims[1, j] = border(sub, low, up, PART, 2, border(sub, low, up, G2))
        rims[2, j] = border(sub, low, up, G3)
    which, at = lax.div(turn, 4), pl.ds(pl.multiple_of(8 * lax.rem(turn, 4), 8), 8)
    chosen = Tiles(lambda j: jnp.where(which == 0, a[at, cols(j)], jnp.where(which == 1, b[at, cols(j)], d[at, cols(j)])))
    for j in range(tiles):
        x, y, z = (chosen[i % tiles] for i in (j - 1, j, j + 1))
        packed[2 * j] = pltpu.roll(jnp.where(lane >= LANES - HALO, x, y), HALO, 1)
        packed[2 * j + 1] = pltpu.roll(jnp.where(lane < HALO, z, y), LANES - HALO, 1)


def residual_kernel(flag, before, initial, start_one, start_two, guess, forcing, coef, rims, packed,
                    messages, ends, two, three, four, one, res, edge, begin):
    tiles = guess.shape[1] // LANES
    lane, sub = iota(1), iota(0)
    first, even = flag[0] == 1, flag[4] == 0
    for j in range(tiles):
        edge[0, j, 0:4, :] = jnp.where(even, start_one[j], start_two[j])
        edge[1, j, 0:4, :] = jnp.where(even, start_two[j], start_one[j])
        for i in (2 * j, 2 * j + 1):
            messages[i, tile(4), :] = packed[i]
    for j in range(tiles):
        low, up = edge[0, j], edge[1, j]
        for r in range(4):
            put(one, j, r, jnp.where(first, initial[tile(r), cols(j)], before[tile(r), cols(j)]))
        put(one, j, 4, border(sub, low, up, START2, 2, border(sub, low, up, START1)))
        begin[0, j] = border(sub, low, up, STEP1, 2, rims[0, j])
        begin[1, j] = rims[1, j] + border(sub, low, up, STEP2, 2)
        begin[2, j] = rims[2, j]

    for inner, (source, target) in enumerate([(one, two), (two, three), (three, four)]):

        def fine(j, r, value, _, inner=inner, target=target):
            put(target, j, r, value + (forcing[inner, tile(r), cols(j)] if r < 4 else begin[inner, j]))

        sweep(source, coef, range(5), fine)

    def last(j, r, value, _):
        value = value + forcing[3, tile(r), cols(j)]
        ends[j, tile(r), :] = value
        res[j, tile(r), :] = value - guess[tile(r), cols(j)]

    sweep(four, coef, range(4), last)

    for r in range(4):
        for j in range(tiles):
            x, y, z = (res[i % tiles, tile(r), :] for i in (j - 1, j, j + 1))
            messages[2 * j, tile(r), :] = pltpu.roll(jnp.where(lane >= LANES - HALO, x, y), HALO, 1)
            messages[2 * j + 1, tile(r), :] = pltpu.roll(jnp.where(lane < HALO, z, y), LANES - HALO, 1)


def chain_kernel(flag, mine, other, messages, coef, one, two):
    pairs = spaces = 8
    rows = spaces * ROWS
    blocks = rows // 8
    lane, sub = iota(1), iota(0)
    zero = jnp.zeros((8, LANES), F32)
    for ref in (one, two):
        ref[0:8, :] = zero
        ref[rows + 8 : rows + 16, :] = zero

    def step(source, t):
        at = 8 * t + 8
        mid = source[at : at + 8, :]
        total = coef[0, tile(t), :] * mid + coef[1, tile(t), :] * source[at - 1 : at + 7, :]
        total += coef[2, tile(t), :] * source[at + 1 : at + 9, :]
        total += coef[3, tile(t), :] * pltpu.roll(mid, 1, 1)
        return total + coef[4, tile(t), :] * pltpu.roll(mid, LANES - 1, 1)

    def emit(pair):
        for s in range(spaces):
            at = 8 + ROWS * s
            tiles = [one[tile(r, at), :] for r in range(4)]
            under, over = slice(at + ROWS, at + ROWS + 8), slice(at - 8, at)
            low_step = pltpu.roll(0.5 * (two[under, :] + one[under, :]), 1, 0)
            up_step = pltpu.roll(0.5 * (two[over, :] + one[over, :]), 7, 0)
            rim = jnp.where(sub < 2, one[under, :], one[over, :])
            rim = jnp.where(sub == 2, low_step, jnp.where(sub == 5, up_step, rim))
            low = [pltpu.roll(x, LANES - HALO, 1) for x in tiles[:3]]
            high = [pltpu.roll(x, HALO, 1) for x in (tiles[3], rim)]
            where = pair * spaces + s
            messages[where, 0:8, :] = jnp.where(lane < 64, low[0], high[0])
            messages[where, 8:16, :] = jnp.where(lane < 64, low[1], high[1])
            messages[where, 16:24, :] = low[2]

    def half():
        for t in range(blocks):
            two[tile(t, 8), :] = step(one, t)

    def run(even):
        sources = (mine, other) if even else (other, mine)

        def arrived(pair, odd, t):
            return sources[int(odd)][pair * spaces + t // 4, tile(t % 4), :]

        def rest(pair, odd):
            for t in range(blocks):
                one[tile(t, 8), :] = step(two, t) + arrived(pair, odd, t)

        for s in range(spaces):
            for r in range(4):
                a, b, d = (sources[r % 2][(4 * i + r) // 2 * spaces + s, tile(4), :] for i in range(3))
                own, up, low, left, right = rates(a, b, d)
                at = tile(r, s * ROWS)
                coef[0, at, :] = 2.0 * own - 1.0
                for i, value in enumerate((up, low, left, right)):
                    coef[i + 1, at, :] = 2.0 * value
        for t in range(blocks):
            one[tile(t, 8), :] = arrived(0, False, t)
        if even:
            for s in range(spaces):
                messages[s] = jnp.zeros((24, LANES), F32)

        def turn(pair, _):
            half()
            if not even:
                emit(pair)
            rest(pair, True)
            half()
            if even:
                emit(pair + 1)
            rest(pair + 1, False)
            return 0

        lax.fori_loop(0, pairs - 1, turn, 0)
        if not even:
            half()
            emit(pairs - 1)

    pl.when(flag[1] == 0)(lambda: run(True))
    pl.when(flag[1] != 0)(lambda: run(False))


def final_kernel(coef, first, second, third, ends, returned, states, err, one, two, extra, out, sems):
    tiles = first.shape[0]
    lane, sub = iota(1), iota(0)
    copies = [pltpu.make_async_copy(out.at[i], states.at[i], sems.at[i]) for i in range(4)]
    for j in range(tiles):
        for r in range(5):
            x, y = returned[2 * j, tile(r % 3), :], returned[2 * j + 1, tile(r % 3), :]
            if r < 3:
                error = jnp.where(lane < 64, x, pltpu.roll(y, 64, 1))
            else:
                error = jnp.where(lane < 64, pltpu.roll(x, 64, 1), y)
            put(err, j, r, error)
        after, behind = pltpu.roll(error, 7, 0), pltpu.roll(error, 1, 0)
        under = after - coef[1, j, tile(4), :] * behind
        over = behind - coef[2, j, tile(4), :] * after
        extra[j] = jnp.where(sub == 1, under, jnp.where(sub == 6, over, 0.0))

    def step_one(j, r, value, _):
        if r < 4:
            out[0, tile(r), cols(j)] = first[j, tile(r, 8), :] + value
        put(one, j, r, value if r < 4 else value + extra[j])

    def step_two(j, r, value, before):
        if r < 4:
            out[1, tile(r), cols(j)] = second[j, tile(r, 8), :] + value
            out[3, tile(r), cols(j)] = ends[j, tile(r), :] + (4.0 * (value - before) + err[j, tile(r, 8), :])
        put(two, j, r, value)

    def step_three(j, r, value, _):
        out[2, tile(r), cols(j)] = third[j, tile(r, 8), :] + value

    sweep(err, coef, range(5), step_one)
    copies[0].start()
    sweep(one, coef, range(5), step_two)
    copies[1].start()
    copies[3].start()
    sweep(two, coef, range(4), step_three)
    copies[2].start()
    for copy in copies:
        copy.wait()


def on_device(guess, forcing, initial, courant_rows, courant_cols, diffusion):
    chips, cores, spaces = (lax.axis_size(n) for n in ("chip", "core", "space"))
    owners = chips * cores
    columns = initial.shape[1]
    tiles = columns // LANES
    everything = ("chip", "core", "space")
    chip, core = lax.axis_index("chip"), lax.axis_index("core")
    turn = chip * cores + core
    flag = jnp.stack([turn == 0, core, turn == owners - 1, turn, lax.axis_index("space") % 2]).astype(jnp.int32)

    def shaped(*shape):
        return jax.ShapeDtypeStruct(shape, F32)

    last = pl.pallas_call(
        last_kernel,
        in_specs=[ANY],
        out_specs=VMEM,
        out_shape=shaped(ROWS, columns),
        scratch_shapes=[pltpu.SemaphoreType.DMA],
        compiler_params=params(52),
        name="last",
    )(guess)
    before = lax.ppermute(last, ("chip", "core"), [(i, i + 1) for i in range(owners - 1)])
    small = pltpu.VMEM((tiles, 8, LANES), F32)
    rim_one, rim_two, start_one, start_two = pl.pallas_call(
        rim_kernel,
        in_specs=[SMEM] + [VMEM] * 5 + [ANY],
        out_specs=[VMEM] * 4,
        out_shape=[shaped(tiles, 8, LANES), shaped(tiles, 8, LANES), shaped(tiles, 4, LANES), shaped(tiles, 4, LANES)],
        scratch_shapes=[pltpu.VMEM((3, 16, columns), F32), pltpu.VMEM((5, tiles, 8, LANES), F32), small, small, small,
                        pltpu.SemaphoreType.DMA((6,))],
        compiler_params=params(52),
        name="rim",
    )(flag, last, initial, courant_rows, courant_cols, diffusion, forcing)

    def exchanged(value, by_turn, first):
        pairs = []
        for k in range(owners):
            for s in range(spaces):
                partner = s + 1 if (s % 2 == 0) == first else s - 1
                if 0 <= partner < spaces:
                    pairs.append((k * spaces + s, (k + by_turn) % owners * spaces + partner))
        return lax.ppermute(value, everything, pairs)

    rim_one, rim_two = exchanged(rim_one, 0, True), exchanged(rim_two, 0, False)
    start_one, start_two = exchanged(start_one, 1, True), exchanged(start_two, 1, False)

    field = pltpu.VMEM((tiles, 48, LANES), F32)
    tall = shaped(tiles, 48, LANES)
    coef, rims, packed = pl.pallas_call(
        prepare_kernel,
        in_specs=[SMEM] + [VMEM] * 5,
        out_specs=[VMEM] * 3,
        out_shape=[shaped(5, tiles, 40, LANES), shaped(3, tiles, 8, LANES), shaped(2 * tiles, 8, LANES)],
        compiler_params=params(20),
        name="prepare",
    )(flag, rim_one, rim_two, courant_rows, courant_cols, diffusion)
    messages, ends, *fields = pl.pallas_call(
        residual_kernel,
        in_specs=[SMEM] + [VMEM] * 9,
        out_specs=[VMEM] * 5,
        out_shape=[shaped(2 * tiles, 40, LANES), shaped(tiles, ROWS, LANES), tall, tall, tall],
        scratch_shapes=[
            field,
            pltpu.VMEM((tiles, ROWS, LANES), F32),
            pltpu.VMEM((2, tiles, 8, LANES), F32),
            pltpu.VMEM((3, tiles, 8, LANES), F32),
        ],
        compiler_params=params(20),
        name="residual",
    )(flag, before, initial, start_one, start_two, last, forcing, coef, rims, packed)

    mine = lax.all_to_all(messages, ("chip", "space"), 0, 0, tiled=True)
    other = lax.ppermute(mine, "core", [(0, 1), (1, 0)])
    rows = spaces * ROWS
    answer = pl.pallas_call(
        chain_kernel,
        in_specs=[SMEM, VMEM, VMEM],
        out_specs=VMEM,
        out_shape=shaped(chips * spaces, 24, LANES),
        scratch_shapes=[
            pltpu.VMEM((5, rows, LANES), F32),
            pltpu.VMEM((rows + 16, LANES), F32),
            pltpu.VMEM((rows + 16, LANES), F32),
        ],
        compiler_params=params(20),
        name="chain",
    )(flag, mine, other)
    returned = lax.all_to_all(answer, ("chip", "space"), 0, 0, tiled=True)
    return pl.pallas_call(
        final_kernel,
        in_specs=[VMEM] * 6,
        out_specs=ANY,
        out_shape=shaped(4, ROWS, columns),
        scratch_shapes=[field, field, field, small, pltpu.VMEM((4, ROWS, columns), F32), pltpu.SemaphoreType.DMA((4,))],
        compiler_params=params(20),
        name="final",
    )(coef, *fields, ends, returned)


def solution(mesh):
    cores = 2
    devices = mesh.devices
    grid = Mesh(
        devices.reshape(devices.shape[0] // cores, cores, devices.shape[1]), ("chip", "core", "space")
    )
    time_rows = P(("chip", "core"), "space", None)
    rows = P("space", None)
    return jax.shard_map(
        on_device,
        mesh=grid,
        in_specs=(time_rows, time_rows, rows, rows, rows, rows),
        out_specs=time_rows,
        check_vma=False,
    )
```

```python
import jax
import jax.numpy as jnp
from jax import lax
from jax.experimental import pallas as pl
from jax.experimental.pallas import tpu as pltpu
from jax.sharding import Mesh, PartitionSpec as P

ROWS = 32
LANES = 128
HALO = 32
VMEM = pl.BlockSpec(memory_space=pltpu.VMEM)
SMEM = pl.BlockSpec(memory_space=pltpu.SMEM)
F32 = jnp.float32
ANY = pl.BlockSpec(memory_space=pl.ANY)
G1, G2, G3, PART, A1, B1, D1, INWARD = range(8)
START1, START2, STEP1, STEP2 = range(4)


def params(mib):
    return pltpu.CompilerParams(vmem_limit_bytes=mib * 1024 * 1024)


def iota(dim):
    return lax.broadcasted_iota(jnp.int32, (8, LANES), dim)


def cols(j):
    return slice(LANES * j, LANES * (j + 1))


def tile(r, first=0):
    return slice(first + 8 * r, first + 8 * r + 8)


def put_pair(ref, i, block, value):
    ref[i, :, cols(block)] = value[0:4]
    ref[i, :, cols(block + 1)] = pltpu.roll(value, 4, 0)[0:4]


def get_pair(ref, i, block):
    return jnp.concatenate([ref[i, :, cols(block)], ref[i, :, cols(block + 1)]], axis=0)


def rates(a, b, d):
    a_pos, a_neg = jnp.maximum(a, 0.0), jnp.minimum(a, 0.0)
    b_pos, b_neg = jnp.maximum(b, 0.0), jnp.minimum(b, 0.0)
    own = 1.0 - (a_pos - a_neg) - (b_pos - b_neg) - 4.0 * d
    return own, d + a_pos, d - a_neg, d + b_pos, d - b_neg


def put(ref, j, r, value):
    ref[j, tile(r, 8), :] = value
    if r == 4:
        ref[j, 0:8, :] = value


def sweep(ref, coef, rows, use):
    tiles = ref.shape[0]
    lane = iota(1)
    for r in rows:
        at = 8 + 8 * r
        mids, rights, lefts = {}, {}, {}

        def load(j):
            j %= tiles
            if j not in mids:
                mids[j] = ref[j, at : at + 8, :]
                rights[j] = pltpu.roll(mids[j], 1, 1)
                lefts[j] = pltpu.roll(mids[j], LANES - 1, 1)

        for j in range(tiles):
            for i in (j - 1, j, j + 1):
                load(i)
            mid = mids[j]
            up = ref[j, at - 1 : at + 7, :]
            low = ref[j, at + 1 : at + 9, :] if r < 4 else ref[j, 1:9, :]
            left = jnp.where(lane == 0, rights[(j - 1) % tiles], rights[j])
            right = jnp.where(lane == LANES - 1, lefts[(j + 1) % tiles], lefts[j])
            total = coef[0, j, tile(r), :] * mid + coef[1, j, tile(r), :] * up
            total += coef[2, j, tile(r), :] * low + coef[3, j, tile(r), :] * left
            use(j, r, total + coef[4, j, tile(r), :] * right, mid)


def last_kernel(guess, last, sem):
    copy = pltpu.make_async_copy(guess.at[3], last, sem)
    copy.start()
    copy.wait()


class Tiles:
    def __init__(self, get):
        self.get, self.seen = get, {}

    def __getitem__(self, j):
        if j not in self.seen:
            self.seen[j] = self.get(j)
        return self.seen[j]


def rim_kernel(flag, last, initial, a, b, d, forcing, rim_one, rim_two, start_one, start_two,
               vg, coef, field, part, after, sems):
    rows, columns = a.shape
    tiles = columns // LANES
    sub, lane = iota(0), iota(1)
    copies = []
    for side, at in enumerate((pl.ds(0, 8), pl.ds(rows - 8, 8))):
        for i in range(3):
            source, target = forcing.at[i, at, :], vg.at[i, pl.ds(8 * side, 8), :]
            copies.append(pltpu.make_async_copy(source, target, sems.at[len(copies)]))
    for copy in copies:
        copy.start()
    at_end, even = flag[2] == 1, flag[4] == 0
    top = sub < 4

    def both(ref, j):
        end = ref.shape[0]
        return jnp.where(top, ref[0:8, cols(j)], ref[end - 8 : end, cols(j)])

    def outward(x):
        return jnp.where(top, pltpu.roll(x, 7, 0), pltpu.roll(x, 1, 0))

    def inward(x):
        return jnp.where(top, pltpu.roll(x, 1, 0), pltpu.roll(x, 7, 0))

    def row(x, side, place, to):
        at = place - 1 if side == 0 else 8 - place
        return pltpu.roll(x, (to - at) % 8, 0)

    OWN, OUT, IN, LEFT, RIGHT = range(5)

    def open_step(values, j):
        x, y, z = (values[i % tiles] for i in (j - 1, j, j + 1))
        left = pltpu.roll(jnp.where(lane == LANES - 1, x, y), 1, 1)
        right = pltpu.roll(jnp.where(lane == 0, z, y), LANES - 1, 1)
        total = coef[OWN, j] * y + coef[OUT, j] * outward(y)
        return total + (coef[LEFT, j] * left + coef[RIGHT, j] * right)

    for j in range(tiles):
        own, upper, lower, left, right = rates(*(both(x, j) for x in (a, b, d)))
        coef[OWN, j], coef[LEFT, j], coef[RIGHT, j] = own, left, right
        coef[OUT, j], coef[IN, j] = jnp.where(top, lower, upper), jnp.where(top, upper, lower)
        field[j] = jnp.where(at_end, both(initial, j), both(last, j))
    values = Tiles(lambda j: field[j])
    for j in range(tiles):
        part[j] = open_step(values, j)
        after[j] = part[j] + coef[IN, j] * inward(values[j])
    for copy in copies:
        copy.wait()
    forced, stepped = Tiles(lambda j: both(vg.at[0], j)), Tiles(lambda j: after[j])
    for j in range(tiles):
        g1, g2, g3 = forced[j], both(vg.at[1], j), both(vg.at[2], j)
        items = [(G1, g1, 1), (G2, g2 + coef[OUT, j] * outward(g1), 1), (G3, g3, 1), (PART, open_step(forced, j) + g2, 2)]
        items += [(A1 + i, both(x, j), 1) for i, x in enumerate((a, b, d))]
        items += [(INWARD, coef[IN, j], 2)]
        values, second = field[j], open_step(stepped, j)
        begins = [(START1, values, 1), (START2, values, 2), (STEP1, part[j], 2), (STEP2, second, 2)]
        rims, starts = [], []
        for side in range(2):
            for found, made in ((items, rims), (begins, starts)):
                total = None
                for to, value, place in found:
                    value = row(value, side, place, to)
                    total = value if total is None else jnp.where(sub == to, value, total)
                made.append(total)
        rim_one[j] = jnp.where(even, rims[1], rims[0])
        rim_two[j] = jnp.where(even, rims[0], rims[1])
        start_one[j] = jnp.where(even, starts[1], starts[0])[0:4]
        start_two[j] = jnp.where(even, starts[0], starts[1])[0:4]


def border(sub, under, over, item, place=1, rest=0.0):
    under = pltpu.roll(under, (place - 1 - item) % 8, 0)
    over = pltpu.roll(over, (8 - place - item) % 8, 0)
    return jnp.where(sub == place - 1, under, jnp.where(sub == 8 - place, over, rest))


def prepare_kernel(flag, rim_one, rim_two, a, b, d, coef, rims, packed):
    tiles = a.shape[1] // LANES
    lane, sub = iota(1), iota(0)
    even, turn = flag[4] == 0, flag[3]
    for j in range(tiles):
        low, up = jnp.where(even, rim_one[j], rim_two[j]), jnp.where(even, rim_two[j], rim_one[j])
        for r in range(4):
            values = a[tile(r), cols(j)], b[tile(r), cols(j)], d[tile(r), cols(j)]
            for i, value in enumerate(rates(*values)):
                coef[i, j, tile(r), :] = value
        own, upper, lower, left, right = rates(*(border(sub, low, up, item) for item in (A1, B1, D1)))
        own = jnp.where((sub == 0) | (sub == 7), own, 0.0)
        upper = jnp.where(sub == 1, pltpu.roll(low, (1 - INWARD) % 8, 0), upper)
        lower = jnp.where(sub == 6, pltpu.roll(up, (6 - INWARD) % 8, 0), lower)
        for i, value in enumerate((own, upper, lower, left, right)):
            coef[i, j, tile(4), :] = value
        rims[0, j] = border(sub, low, up, G1)
        rims[1, j] = border(sub, low, up, PART, 2, border(sub, low, up, G2))
        rims[2, j] = border(sub, low, up, G3)
    at = pl.ds(pl.multiple_of(8 * lax.div(lax.rem(turn, 8), 2), 8), 8)
    later, odd = turn >= 8, lax.rem(turn, 2) == 1

    def choose(j):
        value = jnp.where(later, b[at, cols(j)], a[at, cols(j)])
        return jnp.where(odd, pltpu.roll(value, 4, 0), value)

    chosen = Tiles(choose)
    for j in range(tiles):
        x, y, z = (chosen[i % tiles] for i in (j - 1, j, j + 1))
        packed[2 * j] = pltpu.roll(jnp.where(lane >= LANES - HALO, x, y), HALO, 1)
        packed[2 * j + 1] = pltpu.roll(jnp.where(lane < HALO, z, y), LANES - HALO, 1)


def residual_kernel(flag, before, initial, start_one, start_two, guess, forcing, d, coef, rims, packed,
                    messages, ends, two, three, four, one, res, edge, begin):
    tiles = guess.shape[1] // LANES
    lane, sub = iota(1), iota(0)
    first, even, at_end = flag[0] == 1, flag[4] == 0, flag[2] == 1
    for j in range(tiles):
        edge[0, j, 0:4, :] = jnp.where(even, start_one[j], start_two[j])
        edge[1, j, 0:4, :] = jnp.where(even, start_two[j], start_one[j])
        for i in (2 * j, 2 * j + 1):
            messages[i, :, cols(8)] = packed[i][0:4]
    for j in range(tiles):
        low, up = edge[0, j], edge[1, j]
        for r in range(4):
            put(one, j, r, jnp.where(first, initial[tile(r), cols(j)], before[tile(r), cols(j)]))
        put(one, j, 4, border(sub, low, up, START2, 2, border(sub, low, up, START1)))
        begin[0, j] = border(sub, low, up, STEP1, 2, rims[0, j])
        begin[1, j] = rims[1, j] + border(sub, low, up, STEP2, 2)
        begin[2, j] = rims[2, j]

    for inner, (source, target) in enumerate([(one, two), (two, three), (three, four)]):

        def fine(j, r, value, _, inner=inner, target=target):
            put(target, j, r, value + (forcing[inner, tile(r), cols(j)] if r < 4 else begin[inner, j]))

        sweep(source, coef, range(5), fine)

    def last(j, r, value, _):
        value = value + forcing[3, tile(r), cols(j)]
        ends[j, tile(r), :] = value
        res[j, tile(r), :] = jnp.where(at_end, d[tile(r), cols(j)], value - guess[tile(r), cols(j)])

    sweep(four, coef, range(4), last)

    for r in range(4):
        for j in range(tiles):
            x, y, z = (res[i % tiles, tile(r), :] for i in (j - 1, j, j + 1))
            put_pair(messages, 2 * j, 2 * r, pltpu.roll(jnp.where(lane >= LANES - HALO, x, y), HALO, 1))
            put_pair(messages, 2 * j + 1, 2 * r, pltpu.roll(jnp.where(lane < HALO, z, y), LANES - HALO, 1))


def chain_kernel(flag, mine, other, messages, coef, one, two):
    pairs = spaces = 8
    rows = spaces * ROWS
    blocks = rows // 8
    lane, sub = iota(1), iota(0)
    zero = jnp.zeros((8, LANES), F32)
    for ref in (one, two):
        ref[0:8, :] = zero
        ref[rows + 8 : rows + 16, :] = zero

    def step(source, t):
        at = 8 * t + 8
        mid = source[at : at + 8, :]
        total = coef[0, tile(t), :] * mid + coef[1, tile(t), :] * source[at - 1 : at + 7, :]
        total += coef[2, tile(t), :] * source[at + 1 : at + 9, :]
        total += coef[3, tile(t), :] * pltpu.roll(mid, 1, 1)
        return total + coef[4, tile(t), :] * pltpu.roll(mid, LANES - 1, 1)

    def emit(pair):
        for s in range(spaces):
            at = 8 + ROWS * s
            tiles = [one[tile(r, at), :] for r in range(4)]
            under, over = slice(at + ROWS, at + ROWS + 8), slice(at - 8, at)
            low_step = pltpu.roll(0.5 * (two[under, :] + one[under, :]), 1, 0)
            up_step = pltpu.roll(0.5 * (two[over, :] + one[over, :]), 7, 0)
            rim = jnp.where(sub < 2, one[under, :], one[over, :])
            rim = jnp.where(sub == 2, low_step, jnp.where(sub == 5, up_step, rim))
            low = [pltpu.roll(x, LANES - HALO, 1) for x in tiles[:3]]
            high = [pltpu.roll(x, HALO, 1) for x in (tiles[3], rim)]
            where = pair * spaces + s
            put_pair(messages, where, 0, jnp.where(lane < 64, low[0], high[0]))
            put_pair(messages, where, 2, jnp.where(lane < 64, low[1], high[1]))
            shifted = pltpu.roll(pltpu.roll(tiles[2], 4, 0), HALO, 1)
            messages[where, :, cols(4)] = jnp.where(lane < 64, low[2], shifted)[0:4]

    def half():
        for t in range(blocks):
            two[tile(t, 8), :] = step(one, t)

    def run(even):
        sources = (mine, other) if even else (other, mine)

        def arrived(pair, odd, t):
            return get_pair(sources[int(odd)], pair * spaces + t // 4, 2 * (t % 4))

        def rest(pair, odd):
            for t in range(blocks):
                one[tile(t, 8), :] = step(two, t) + arrived(pair, odd, t)

        for s in range(spaces):
            for r in range(4):
                a, b = (
                    jnp.concatenate([x[(4 * i + r) * spaces + s, :, cols(8)] for x in sources], axis=0) for i in range(2)
                )
                d = arrived(pairs - 1, True, 4 * s + r)
                own, up, low, left, right = rates(a, b, d)
                at = tile(r, s * ROWS)
                coef[0, at, :] = 2.0 * own - 1.0
                for i, value in enumerate((up, low, left, right)):
                    coef[i + 1, at, :] = 2.0 * value
        for t in range(blocks):
            one[tile(t, 8), :] = arrived(0, False, t)
        if even:
            for s in range(spaces):
                messages[s] = jnp.zeros((4, 5 * LANES), F32)

        def turn(pair, _):
            half()
            if not even:
                emit(pair)
            rest(pair, True)
            half()
            if even:
                emit(pair + 1)
            rest(pair + 1, False)
            return 0

        lax.fori_loop(0, pairs - 1, turn, 0)
        if not even:
            half()
            emit(pairs - 1)

    pl.when(flag[1] == 0)(lambda: run(True))
    pl.when(flag[1] != 0)(lambda: run(False))


def final_kernel(coef, first, second, third, ends, returned, states, err, one, two, extra, out, sems):
    tiles = first.shape[0]
    lane, sub = iota(1), iota(0)
    copies = [pltpu.make_async_copy(out.at[i], states.at[i], sems.at[i]) for i in range(4)]
    for j in range(tiles):
        for r in range(5):
            if r == 2:
                x, y = (jnp.concatenate([returned[i, :, cols(4)]] * 2, axis=0) for i in (2 * j, 2 * j + 1))
                upper = jnp.where(lane < 64, x, pltpu.roll(y, 64, 1))
                error = jnp.where(sub < 4, upper, jnp.where(lane < 64, pltpu.roll(x, 64, 1), y))
            else:
                x, y = (get_pair(returned, i, 2 * (r % 3)) for i in (2 * j, 2 * j + 1))
                if r < 3:
                    error = jnp.where(lane < 64, x, pltpu.roll(y, 64, 1))
                else:
                    error = jnp.where(lane < 64, pltpu.roll(x, 64, 1), y)
            put(err, j, r, error)
        after, behind = pltpu.roll(error, 7, 0), pltpu.roll(error, 1, 0)
        under = after - coef[1, j, tile(4), :] * behind
        over = behind - coef[2, j, tile(4), :] * after
        extra[j] = jnp.where(sub == 1, under, jnp.where(sub == 6, over, 0.0))

    def step_one(j, r, value, _):
        if r < 4:
            out[0, tile(r), cols(j)] = first[j, tile(r, 8), :] + value
        put(one, j, r, value if r < 4 else value + extra[j])

    def step_two(j, r, value, before):
        if r < 4:
            out[1, tile(r), cols(j)] = second[j, tile(r, 8), :] + value
            out[3, tile(r), cols(j)] = ends[j, tile(r), :] + (4.0 * (value - before) + err[j, tile(r, 8), :])
        put(two, j, r, value)

    def step_three(j, r, value, _):
        out[2, tile(r), cols(j)] = third[j, tile(r, 8), :] + value

    sweep(err, coef, range(5), step_one)
    copies[0].start()
    sweep(one, coef, range(5), step_two)
    copies[1].start()
    copies[3].start()
    sweep(two, coef, range(4), step_three)
    copies[2].start()
    for copy in copies:
        copy.wait()


def on_device(guess, forcing, initial, courant_rows, courant_cols, diffusion):
    chips, cores, spaces = (lax.axis_size(n) for n in ("chip", "core", "space"))
    owners = chips * cores
    columns = initial.shape[1]
    tiles = columns // LANES
    everything = ("chip", "core", "space")
    chip, core = lax.axis_index("chip"), lax.axis_index("core")
    turn = chip * cores + core
    flag = jnp.stack([turn == 0, core, turn == owners - 1, turn, lax.axis_index("space") % 2]).astype(jnp.int32)

    def shaped(*shape):
        return jax.ShapeDtypeStruct(shape, F32)

    last = pl.pallas_call(
        last_kernel,
        in_specs=[ANY],
        out_specs=VMEM,
        out_shape=shaped(ROWS, columns),
        scratch_shapes=[pltpu.SemaphoreType.DMA],
        compiler_params=params(52),
        name="last",
    )(guess)
    before = lax.ppermute(last, ("chip", "core"), [(i, i + 1) for i in range(owners - 1)])
    small = pltpu.VMEM((tiles, 8, LANES), F32)
    rim_one, rim_two, start_one, start_two = pl.pallas_call(
        rim_kernel,
        in_specs=[SMEM] + [VMEM] * 5 + [ANY],
        out_specs=[VMEM] * 4,
        out_shape=[shaped(tiles, 8, LANES), shaped(tiles, 8, LANES), shaped(tiles, 4, LANES), shaped(tiles, 4, LANES)],
        scratch_shapes=[pltpu.VMEM((3, 16, columns), F32), pltpu.VMEM((5, tiles, 8, LANES), F32), small, small, small,
                        pltpu.SemaphoreType.DMA((6,))],
        compiler_params=params(52),
        name="rim",
    )(flag, last, initial, courant_rows, courant_cols, diffusion, forcing)

    def exchanged(value, by_turn, first):
        pairs = []
        for k in range(owners):
            for s in range(spaces):
                partner = s + 1 if (s % 2 == 0) == first else s - 1
                if 0 <= partner < spaces:
                    pairs.append((k * spaces + s, (k + by_turn) % owners * spaces + partner))
        return lax.ppermute(value, everything, pairs)

    rim_one, rim_two = exchanged(rim_one, 0, True), exchanged(rim_two, 0, False)
    start_one, start_two = exchanged(start_one, 1, True), exchanged(start_two, 1, False)

    field = pltpu.VMEM((tiles, 48, LANES), F32)
    tall = shaped(tiles, 48, LANES)
    coef, rims, packed = pl.pallas_call(
        prepare_kernel,
        in_specs=[SMEM] + [VMEM] * 5,
        out_specs=[VMEM] * 3,
        out_shape=[shaped(5, tiles, 40, LANES), shaped(3, tiles, 8, LANES), shaped(2 * tiles, 8, LANES)],
        compiler_params=params(20),
        name="prepare",
    )(flag, rim_one, rim_two, courant_rows, courant_cols, diffusion)
    messages, ends, *fields = pl.pallas_call(
        residual_kernel,
        in_specs=[SMEM] + [VMEM] * 10,
        out_specs=[VMEM] * 5,
        out_shape=[shaped(2 * tiles, 4, 9 * LANES), shaped(tiles, ROWS, LANES), tall, tall, tall],
        scratch_shapes=[
            field,
            pltpu.VMEM((tiles, ROWS, LANES), F32),
            pltpu.VMEM((2, tiles, 8, LANES), F32),
            pltpu.VMEM((3, tiles, 8, LANES), F32),
        ],
        compiler_params=params(20),
        name="residual",
    )(flag, before, initial, start_one, start_two, last, forcing, diffusion, coef, rims, packed)

    mine = lax.all_to_all(messages, ("chip", "space"), 0, 0, tiled=True)
    other = lax.ppermute(mine, "core", [(0, 1), (1, 0)])
    rows = spaces * ROWS
    answer = pl.pallas_call(
        chain_kernel,
        in_specs=[SMEM, VMEM, VMEM],
        out_specs=VMEM,
        out_shape=shaped(chips * spaces, 4, 5 * LANES),
        scratch_shapes=[
            pltpu.VMEM((5, rows, LANES), F32),
            pltpu.VMEM((rows + 16, LANES), F32),
            pltpu.VMEM((rows + 16, LANES), F32),
        ],
        compiler_params=params(20),
        name="chain",
    )(flag, mine, other)
    returned = lax.all_to_all(answer, ("chip", "space"), 0, 0, tiled=True)
    return pl.pallas_call(
        final_kernel,
        in_specs=[VMEM] * 6,
        out_specs=ANY,
        out_shape=shaped(4, ROWS, columns),
        scratch_shapes=[field, field, field, small, pltpu.VMEM((4, ROWS, columns), F32), pltpu.SemaphoreType.DMA((4,))],
        compiler_params=params(20),
        name="final",
    )(coef, *fields, ends, returned)


def solution(mesh):
    cores = 2
    devices = mesh.devices
    grid = Mesh(
        devices.reshape(devices.shape[0] // cores, cores, devices.shape[1]), ("chip", "core", "space")
    )
    time_rows = P(("chip", "core"), "space", None)
    rows = P("space", None)
    return jax.shard_map(
        on_device,
        mesh=grid,
        in_specs=(time_rows, time_rows, rows, rows, rows, rows),
        out_specs=time_rows,
        check_vma=False,
    )
```

```python
import jax
import jax.numpy as jnp
from jax import lax
from jax.experimental import pallas as pl
from jax.experimental.pallas import tpu as pltpu
from jax.sharding import Mesh, PartitionSpec as P

ROWS = 32
LANES = 128
HALO = 32
VMEM = pl.BlockSpec(memory_space=pltpu.VMEM)
SMEM = pl.BlockSpec(memory_space=pltpu.SMEM)
F32 = jnp.float32
ANY = pl.BlockSpec(memory_space=pl.ANY)
G1, PART, G2, INWARD, G3, A1, B1, D1 = range(8)
START1, START2, STEP1, STEP2 = range(4)


def params(mib):
    return pltpu.CompilerParams(vmem_limit_bytes=mib * 1024 * 1024)


def iota(dim):
    return lax.broadcasted_iota(jnp.int32, (8, LANES), dim)


def cols(j):
    return slice(LANES * j, LANES * (j + 1))


def tile(r, first=0):
    return slice(first + 8 * r, first + 8 * r + 8)


def put_pair(ref, i, block, value):
    ref[i, :, cols(block)] = value[0:4]
    ref[i, :, cols(block + 1)] = pltpu.roll(value, 4, 0)[0:4]


def get_pair(ref, i, block):
    return jnp.concatenate([ref[i, :, cols(block)], ref[i, :, cols(block + 1)]], axis=0)


def rates(a, b, d):
    a_pos, a_neg = jnp.maximum(a, 0.0), jnp.minimum(a, 0.0)
    b_pos, b_neg = jnp.maximum(b, 0.0), jnp.minimum(b, 0.0)
    own = 1.0 - (a_pos - a_neg) - (b_pos - b_neg) - 4.0 * d
    return own, d + a_pos, d - a_neg, d + b_pos, d - b_neg


def put(ref, j, r, value):
    ref[j, tile(r, 8), :] = value
    if r == 4:
        ref[j, 0:8, :] = value


def sweep(ref, coef, rows, use):
    tiles = ref.shape[0]
    lane = iota(1)
    for r in rows:
        at = 8 + 8 * r
        mids, rights, lefts = {}, {}, {}

        def load(j):
            j %= tiles
            if j not in mids:
                mids[j] = ref[j, at : at + 8, :]
                rights[j] = pltpu.roll(mids[j], 1, 1)
                lefts[j] = pltpu.roll(mids[j], LANES - 1, 1)

        for j in range(tiles):
            for i in (j - 1, j, j + 1):
                load(i)
            mid = mids[j]
            up = ref[j, at - 1 : at + 7, :]
            low = ref[j, at + 1 : at + 9, :] if r < 4 else ref[j, 1:9, :]
            left = jnp.where(lane == 0, rights[(j - 1) % tiles], rights[j])
            right = jnp.where(lane == LANES - 1, lefts[(j + 1) % tiles], lefts[j])
            total = coef[0, j, tile(r), :] * mid + coef[1, j, tile(r), :] * up
            total += coef[2, j, tile(r), :] * low + coef[3, j, tile(r), :] * left
            use(j, r, total + coef[4, j, tile(r), :] * right, mid)


def last_kernel(guess, last, sem):
    copy = pltpu.make_async_copy(guess.at[3], last, sem)
    copy.start()
    copy.wait()


class Tiles:
    def __init__(self, get):
        self.get, self.seen = get, {}

    def __getitem__(self, j):
        if j not in self.seen:
            self.seen[j] = self.get(j)
        return self.seen[j]


def rim_kernel(flag, last, initial, a, b, d, forcing, rim_one, rim_two, start_one, start_two,
               vg, coef, field, part, after, sems):
    rows, columns = a.shape
    tiles = columns // LANES
    sub, lane = iota(0), iota(1)
    copies = []
    for side, at in enumerate((pl.ds(0, 8), pl.ds(rows - 8, 8))):
        for i in range(3):
            source, target = forcing.at[i, at, :], vg.at[i, pl.ds(8 * side, 8), :]
            copies.append(pltpu.make_async_copy(source, target, sems.at[len(copies)]))
    for copy in copies:
        copy.start()
    at_end, even = flag[2] == 1, flag[4] == 0
    top = sub < 4

    def both(ref, j):
        end = ref.shape[0]
        return jnp.where(top, ref[0:8, cols(j)], ref[end - 8 : end, cols(j)])

    def outward(x):
        return jnp.where(top, pltpu.roll(x, 7, 0), pltpu.roll(x, 1, 0))

    def inward(x):
        return jnp.where(top, pltpu.roll(x, 1, 0), pltpu.roll(x, 7, 0))

    second_row = (sub == 1) | (sub == 6)

    def collect(pieces, side):
        total = None
        for value, by in pieces:
            if by:
                value = pltpu.roll(value, by if side == 0 else 8 - by, 0)
            here = sub >= by if side == 0 else sub <= 7 - by
            total = value if total is None else jnp.where(here, value, total)
        return total

    def start_rows(pieces, side):
        (values, _), (first, by), (second, far) = pieces
        ways = [by, far] if side == 0 else [8 - by, 8 - far]
        first, second = (pltpu.roll(x, way, 0) for x, way in zip((first, second), ways, strict=True))
        places = (STEP1, STEP2) if side == 0 else (7 - STEP1, 7 - STEP2)
        total = jnp.where(sub == places[0], first, jnp.where(sub == places[1], second, values))
        return total if side == 0 else pltpu.roll(total, 4, 0)

    OWN, OUT, IN, LEFT, RIGHT = range(5)

    def open_step(values, j):
        x, y, z = (values[i % tiles] for i in (j - 1, j, j + 1))
        left = pltpu.roll(jnp.where(lane == LANES - 1, x, y), 1, 1)
        right = pltpu.roll(jnp.where(lane == 0, z, y), LANES - 1, 1)
        total = coef[OWN, j] * y + coef[OUT, j] * outward(y)
        return total + (coef[LEFT, j] * left + coef[RIGHT, j] * right)

    for j in range(tiles):
        own, upper, lower, left, right = rates(*(both(x, j) for x in (a, b, d)))
        coef[OWN, j], coef[LEFT, j], coef[RIGHT, j] = own, left, right
        coef[OUT, j], coef[IN, j] = jnp.where(top, lower, upper), jnp.where(top, upper, lower)
        field[j] = jnp.where(at_end, both(initial, j), both(last, j))
    values = Tiles(lambda j: field[j])
    for j in range(tiles):
        part[j] = open_step(values, j)
        after[j] = part[j] + coef[IN, j] * inward(values[j])
    for copy in copies:
        copy.wait()
    forced, stepped = Tiles(lambda j: both(vg.at[0], j)), Tiles(lambda j: after[j])
    for j in range(tiles):
        g1, g2, g3 = forced[j], both(vg.at[1], j), both(vg.at[2], j)
        second = open_step(stepped, j)
        forced_rows = jnp.where(second_row, open_step(forced, j) + g2, g1)
        mixed_rows = jnp.where(second_row, coef[IN, j], g2 + coef[OUT, j] * outward(g1))
        pieces = [(forced_rows, G1), (mixed_rows, G2), (g3, G3)]
        pieces += [(both(x, j), to) for x, to in ((a, A1), (b, B1), (d, D1))]
        begins = [(field[j], START1), (part[j], STEP1 - 1), (second, STEP2 - 1)]
        rims = [collect(pieces, side) for side in range(2)]
        starts = [start_rows(begins, side) for side in range(2)]
        rim_one[j] = jnp.where(even, rims[1], rims[0])
        rim_two[j] = jnp.where(even, rims[0], rims[1])
        start_one[j] = jnp.where(even, starts[1], starts[0])[0:4]
        start_two[j] = jnp.where(even, starts[0], starts[1])[0:4]


def border(sub, under, over, item, place=1, rest=0.0):
    under = pltpu.roll(under, (place - 1 - item) % 8, 0)
    over = pltpu.roll(over, (1 - place + item) % 8, 0)
    return jnp.where(sub == place - 1, under, jnp.where(sub == 8 - place, over, rest))


def prepare_kernel(flag, rim_one, rim_two, a, b, d, coef, rims, packed):
    tiles = a.shape[1] // LANES
    lane, sub = iota(1), iota(0)
    even, turn = flag[4] == 0, flag[3]
    for j in range(tiles):
        low, up = jnp.where(even, rim_one[j], rim_two[j]), jnp.where(even, rim_two[j], rim_one[j])
        for r in range(4):
            values = a[tile(r), cols(j)], b[tile(r), cols(j)], d[tile(r), cols(j)]
            for i, value in enumerate(rates(*values)):
                coef[i, j, tile(r), :] = value
        own, upper, lower, left, right = rates(*(border(sub, low, up, item) for item in (A1, B1, D1)))
        own = jnp.where((sub == 0) | (sub == 7), own, 0.0)
        upper = jnp.where(sub == 1, pltpu.roll(low, (1 - INWARD) % 8, 0), upper)
        lower = jnp.where(sub == 6, pltpu.roll(up, (INWARD - 1) % 8, 0), lower)
        for i, value in enumerate((own, upper, lower, left, right)):
            coef[i, j, tile(4), :] = value
        rims[0, j] = border(sub, low, up, G1)
        rims[1, j] = border(sub, low, up, PART, 2, border(sub, low, up, G2))
        rims[2, j] = border(sub, low, up, G3)
    at = pl.ds(pl.multiple_of(8 * lax.div(lax.rem(turn, 8), 2), 8), 8)
    later, odd = turn >= 8, lax.rem(turn, 2) == 1

    def choose(j):
        value = jnp.where(later, b[at, cols(j)], a[at, cols(j)])
        return jnp.where(odd, pltpu.roll(value, 4, 0), value)

    chosen = Tiles(choose)
    for j in range(tiles):
        x, y, z = (chosen[i % tiles] for i in (j - 1, j, j + 1))
        packed[2 * j] = pltpu.roll(jnp.where(lane >= LANES - HALO, x, y), HALO, 1)
        packed[2 * j + 1] = pltpu.roll(jnp.where(lane < HALO, z, y), LANES - HALO, 1)


def residual_kernel(flag, before, initial, start_one, start_two, guess, forcing, d, coef, rims, packed,
                    messages, ends, two, three, four, one, res, edge, begin):
    tiles = guess.shape[1] // LANES
    lane, sub = iota(1), iota(0)
    first, even, at_end = flag[0] == 1, flag[4] == 0, flag[2] == 1
    for j in range(tiles):
        edge[0, j, 0:4, :] = jnp.where(even, start_one[j], start_two[j])
        edge[1, j, 4:8, :] = jnp.where(even, start_two[j], start_one[j])
        for i in (2 * j, 2 * j + 1):
            messages[i, :, cols(8)] = packed[i][0:4]
    for j in range(tiles):
        low, up = edge[0, j], edge[1, j]
        for r in range(4):
            put(one, j, r, jnp.where(first, initial[tile(r), cols(j)], before[tile(r), cols(j)]))
        put(one, j, 4, border(sub, low, up, START2, 2, border(sub, low, up, START1)))
        begin[0, j] = border(sub, low, up, STEP1, 2, rims[0, j])
        begin[1, j] = rims[1, j] + border(sub, low, up, STEP2, 2)
        begin[2, j] = rims[2, j]

    for inner, (source, target) in enumerate([(one, two), (two, three), (three, four)]):

        def fine(j, r, value, _, inner=inner, target=target):
            put(target, j, r, value + (forcing[inner, tile(r), cols(j)] if r < 4 else begin[inner, j]))

        sweep(source, coef, range(5), fine)

    def last(j, r, value, _):
        value = value + forcing[3, tile(r), cols(j)]
        ends[j, tile(r), :] = value
        res[j, tile(r), :] = jnp.where(at_end, d[tile(r), cols(j)], value - guess[tile(r), cols(j)])

    sweep(four, coef, range(4), last)

    for r in range(4):
        for j in range(tiles):
            x, y, z = (res[i % tiles, tile(r), :] for i in (j - 1, j, j + 1))
            put_pair(messages, 2 * j, 2 * r, pltpu.roll(jnp.where(lane >= LANES - HALO, x, y), HALO, 1))
            put_pair(messages, 2 * j + 1, 2 * r, pltpu.roll(jnp.where(lane < HALO, z, y), LANES - HALO, 1))


def chain_kernel(flag, mine, other, messages, coef, one, two):
    pairs = spaces = 8
    rows = spaces * ROWS
    blocks = rows // 8
    lane, sub = iota(1), iota(0)
    zero = jnp.zeros((8, LANES), F32)
    for ref in (one, two):
        ref[0:8, :] = zero
        ref[rows + 8 : rows + 16, :] = zero

    def step(source, t):
        at = 8 * t + 8
        mid = source[at : at + 8, :]
        total = coef[0, tile(t), :] * mid + coef[1, tile(t), :] * source[at - 1 : at + 7, :]
        total += coef[2, tile(t), :] * source[at + 1 : at + 9, :]
        total += coef[3, tile(t), :] * pltpu.roll(mid, 1, 1)
        return total + coef[4, tile(t), :] * pltpu.roll(mid, LANES - 1, 1)

    def emit(pair):
        for s in range(spaces):
            at = 8 + ROWS * s
            tiles = [one[tile(r, at), :] for r in range(4)]
            under, over = slice(at + ROWS, at + ROWS + 8), slice(at - 8, at)
            low_step = pltpu.roll(0.5 * (two[under, :] + one[under, :]), 1, 0)
            up_step = pltpu.roll(0.5 * (two[over, :] + one[over, :]), 7, 0)
            rim = jnp.where(sub < 2, one[under, :], one[over, :])
            rim = jnp.where(sub == 2, low_step, jnp.where(sub == 5, up_step, rim))
            low = [pltpu.roll(x, LANES - HALO, 1) for x in tiles[:3]]
            high = [pltpu.roll(x, HALO, 1) for x in (tiles[3], rim)]
            where = pair * spaces + s
            put_pair(messages, where, 0, jnp.where(lane < 64, low[0], high[0]))
            put_pair(messages, where, 2, jnp.where(lane < 64, low[1], high[1]))
            shifted = pltpu.roll(pltpu.roll(tiles[2], 4, 0), HALO, 1)
            messages[where, :, cols(4)] = jnp.where(lane < 64, low[2], shifted)[0:4]

    def half():
        for t in range(blocks):
            two[tile(t, 8), :] = step(one, t)

    def run(even):
        sources = (mine, other) if even else (other, mine)

        def arrived(pair, odd, t):
            return get_pair(sources[int(odd)], pair * spaces + t // 4, 2 * (t % 4))

        def rest(pair, odd):
            for t in range(blocks):
                one[tile(t, 8), :] = step(two, t) + arrived(pair, odd, t)

        for s in range(spaces):
            for r in range(4):
                a, b = (
                    jnp.concatenate([x[(4 * i + r) * spaces + s, :, cols(8)] for x in sources], axis=0) for i in range(2)
                )
                d = arrived(pairs - 1, True, 4 * s + r)
                own, up, low, left, right = rates(a, b, d)
                at = tile(r, s * ROWS)
                coef[0, at, :] = 2.0 * own - 1.0
                for i, value in enumerate((up, low, left, right)):
                    coef[i + 1, at, :] = 2.0 * value
        for t in range(blocks):
            one[tile(t, 8), :] = arrived(0, False, t)
        if even:
            for s in range(spaces):
                messages[s] = jnp.zeros((4, 5 * LANES), F32)

        def turn(pair):
            half()
            if not even:
                emit(pair)
            rest(pair, True)
            half()
            if even:
                emit(pair + 1)
            rest(pair + 1, False)

        for pair in range(pairs - 1):
            turn(pair)
        if not even:
            half()
            emit(pairs - 1)

    pl.when(flag[1] == 0)(lambda: run(True))
    pl.when(flag[1] != 0)(lambda: run(False))


def final_kernel(coef, first, second, third, ends, returned, states, err, one, two, extra, out, sems):
    tiles = first.shape[0]
    lane, sub = iota(1), iota(0)
    copies = [pltpu.make_async_copy(out.at[i], states.at[i], sems.at[i]) for i in range(4)]
    for j in range(tiles):
        for r in range(5):
            if r == 2:
                x, y = (jnp.concatenate([returned[i, :, cols(4)]] * 2, axis=0) for i in (2 * j, 2 * j + 1))
                upper = jnp.where(lane < 64, x, pltpu.roll(y, 64, 1))
                error = jnp.where(sub < 4, upper, jnp.where(lane < 64, pltpu.roll(x, 64, 1), y))
            else:
                x, y = (get_pair(returned, i, 2 * (r % 3)) for i in (2 * j, 2 * j + 1))
                if r < 3:
                    error = jnp.where(lane < 64, x, pltpu.roll(y, 64, 1))
                else:
                    error = jnp.where(lane < 64, pltpu.roll(x, 64, 1), y)
            put(err, j, r, error)
        after, behind = pltpu.roll(error, 7, 0), pltpu.roll(error, 1, 0)
        under = after - coef[1, j, tile(4), :] * behind
        over = behind - coef[2, j, tile(4), :] * after
        extra[j] = jnp.where(sub == 1, under, jnp.where(sub == 6, over, 0.0))

    def step_one(j, r, value, _):
        if r < 4:
            out[0, tile(r), cols(j)] = first[j, tile(r, 8), :] + value
        put(one, j, r, value if r < 4 else value + extra[j])

    def step_two(j, r, value, before):
        if r < 4:
            out[1, tile(r), cols(j)] = second[j, tile(r, 8), :] + value
            out[3, tile(r), cols(j)] = ends[j, tile(r), :] + (4.0 * (value - before) + err[j, tile(r, 8), :])
        put(two, j, r, value)

    def step_three(j, r, value, _):
        out[2, tile(r), cols(j)] = third[j, tile(r, 8), :] + value

    sweep(err, coef, range(5), step_one)
    copies[0].start()
    sweep(one, coef, range(5), step_two)
    copies[1].start()
    copies[3].start()
    sweep(two, coef, range(4), step_three)
    copies[2].start()
    for copy in copies:
        copy.wait()


def on_device(guess, forcing, initial, courant_rows, courant_cols, diffusion):
    chips, cores, spaces = (lax.axis_size(n) for n in ("chip", "core", "space"))
    owners = chips * cores
    columns = initial.shape[1]
    tiles = columns // LANES
    everything = ("chip", "core", "space")
    chip, core = lax.axis_index("chip"), lax.axis_index("core")
    turn = chip * cores + core
    flag = jnp.stack([turn == 0, core, turn == owners - 1, turn, lax.axis_index("space") % 2]).astype(jnp.int32)

    def shaped(*shape):
        return jax.ShapeDtypeStruct(shape, F32)

    last = pl.pallas_call(
        last_kernel,
        in_specs=[ANY],
        out_specs=VMEM,
        out_shape=shaped(ROWS, columns),
        scratch_shapes=[pltpu.SemaphoreType.DMA],
        compiler_params=params(52),
        name="last",
    )(guess)
    before = lax.ppermute(last, ("chip", "core"), [(i, i + 1) for i in range(owners - 1)])
    small = pltpu.VMEM((tiles, 8, LANES), F32)
    rim_one, rim_two, start_one, start_two = pl.pallas_call(
        rim_kernel,
        in_specs=[SMEM] + [VMEM] * 5 + [ANY],
        out_specs=[VMEM] * 4,
        out_shape=[shaped(tiles, 8, LANES), shaped(tiles, 8, LANES), shaped(tiles, 4, LANES), shaped(tiles, 4, LANES)],
        scratch_shapes=[pltpu.VMEM((3, 16, columns), F32), pltpu.VMEM((5, tiles, 8, LANES), F32), small, small, small,
                        pltpu.SemaphoreType.DMA((6,))],
        compiler_params=params(52),
        name="rim",
    )(flag, last, initial, courant_rows, courant_cols, diffusion, forcing)

    def exchanged(value, by_turn, first):
        pairs = []
        for k in range(owners):
            for s in range(spaces):
                partner = s + 1 if (s % 2 == 0) == first else s - 1
                if 0 <= partner < spaces:
                    pairs.append((k * spaces + s, (k + by_turn) % owners * spaces + partner))
        return lax.ppermute(value, everything, pairs)

    rim_one, rim_two = exchanged(rim_one, 0, True), exchanged(rim_two, 0, False)
    start_one, start_two = exchanged(start_one, 1, True), exchanged(start_two, 1, False)

    field = pltpu.VMEM((tiles, 48, LANES), F32)
    tall = shaped(tiles, 48, LANES)
    coef, rims, packed = pl.pallas_call(
        prepare_kernel,
        in_specs=[SMEM] + [VMEM] * 5,
        out_specs=[VMEM] * 3,
        out_shape=[shaped(5, tiles, 40, LANES), shaped(3, tiles, 8, LANES), shaped(2 * tiles, 8, LANES)],
        compiler_params=params(20),
        name="prepare",
    )(flag, rim_one, rim_two, courant_rows, courant_cols, diffusion)
    messages, ends, *fields = pl.pallas_call(
        residual_kernel,
        in_specs=[SMEM] + [VMEM] * 10,
        out_specs=[VMEM] * 5,
        out_shape=[shaped(2 * tiles, 4, 9 * LANES), shaped(tiles, ROWS, LANES), tall, tall, tall],
        scratch_shapes=[
            field,
            pltpu.VMEM((tiles, ROWS, LANES), F32),
            pltpu.VMEM((2, tiles, 8, LANES), F32),
            pltpu.VMEM((3, tiles, 8, LANES), F32),
        ],
        compiler_params=params(20),
        name="residual",
    )(flag, before, initial, start_one, start_two, last, forcing, diffusion, coef, rims, packed)

    mine = lax.all_to_all(messages, ("chip", "space"), 0, 0, tiled=True)
    other = lax.ppermute(mine, "core", [(0, 1), (1, 0)])
    rows = spaces * ROWS
    answer = pl.pallas_call(
        chain_kernel,
        in_specs=[SMEM, VMEM, VMEM],
        out_specs=VMEM,
        out_shape=shaped(chips * spaces, 4, 5 * LANES),
        scratch_shapes=[
            pltpu.VMEM((5, rows, LANES), F32),
            pltpu.VMEM((rows + 16, LANES), F32),
            pltpu.VMEM((rows + 16, LANES), F32),
        ],
        compiler_params=params(20),
        name="chain",
    )(flag, mine, other)
    returned = lax.all_to_all(answer, ("chip", "space"), 0, 0, tiled=True)
    return pl.pallas_call(
        final_kernel,
        in_specs=[VMEM] * 6,
        out_specs=ANY,
        out_shape=shaped(4, ROWS, columns),
        scratch_shapes=[field, field, field, small, pltpu.VMEM((4, ROWS, columns), F32), pltpu.SemaphoreType.DMA((4,))],
        compiler_params=params(20),
        name="final",
    )(coef, *fields, ends, returned)


def solution(mesh):
    cores = 2
    devices = mesh.devices
    grid = Mesh(
        devices.reshape(devices.shape[0] // cores, cores, devices.shape[1]), ("chip", "core", "space")
    )
    time_rows = P(("chip", "core"), "space", None)
    rows = P("space", None)
    return jax.shard_map(
        on_device,
        mesh=grid,
        in_specs=(time_rows, time_rows, rows, rows, rows, rows),
        out_specs=time_rows,
        check_vma=False,
    )
```
